32 devices in a mesh: gx: 4 (over y, core), gy: 8 (over z, x).
Axes of the slice: x: 2, y: 2, z: 4, core: 2. Of those that a mesh axis runs over, the one named last changes fastest.
Arguments:
- rhs: float32 [32, 64, 512], P('gx', 'gy'), may hold values from -18 to 18
- diag: float32 [32, 64, 512], P('gx', 'gy'), may hold values from 0.5 to 2
- smoother_center: float32 [32, 64, 512], P('gx', 'gy'), may hold values from 0.1 to 0.2
- smoother_faces: float32 [6, 32, 64, 512], P(None, 'gx', 'gy'), may hold values from 0.01 to 0.05
- send_count: int32 [4, 8, 8], P('gx', 'gy'), may hold values from 0 to 4096, as said below
- send_cell: int32 [4, 8, 8, 4096], P('gx', 'gy'), may hold values from 0 to 32767, as said below
- restrict_col: int32 [27, 4, 8, 4096], P(None, 'gx', 'gy'), may hold values from 0 to 65535, as said below
- restrict_vals: float32 [27, 4, 8, 4096], P(None, 'gx', 'gy'), may hold values from 0.03 to 0.2
- coarse_col: int32 [16, 4, 8, 4096], P(None, 'gx', 'gy'), may hold values from 0 to 12287, as said below
- coarse_diag: float32 [4, 8, 4096], P('gx', 'gy'), may hold values from 3 to 6
- coarse_vals: float32 [16, 4, 8, 4096], P(None, 'gx', 'gy'), may hold values from -3 to 3
- csmooth_diag: float32 [4, 8, 4096], P('gx', 'gy'), may hold values from 0.15 to 0.3
- csmooth_vals: float32 [16, 4, 8, 4096], P(None, 'gx', 'gy'), may hold values from -0.3 to 0.3
- remote_row: int32 [4, 4, 8, 8, 4096], P(None, 'gx', 'gy'), may hold values from 0 to 4095, as said below
- remote_vals: float32 [4, 4, 8, 8, 4096], P(None, 'gx', 'gy'), may hold values from 0.3 to 1
- interp_row: int32 [4, 32, 64, 512], P(None, 'gx', 'gy'), may hold values from 0 to 4095, as said below
- interp_vals: float32 [4, 32, 64, 512], P(None, 'gx', 'gy'), may hold values from 0.3 to 1
Outputs:
- solution: float32 [32, 64, 512], P('gx', 'gy')
- residual: float32 [32, 64, 512], P('gx', 'gy')
The draws below stay inside these ranges and needn't reach their ends.
Inputs may be any that keep to these rules, and one draw needn't show every extreme that they name: `send_count`: zero towards a neighbour outside the grid; one device receives 4096 used slots from each of its eight neighbours, and about a quarter of the devices receive several times more than the rest. `send_cell`: the cell of a slot towards direction d lies within 2 cells of the side facing that neighbour, within 4 cells of both sides for a diagonal neighbour. The slots of one direction in one aligned block of 128 slots lie in one run of 128 cells along z that starts at a multiple of 128. `restrict_col`: only a device's first 1024 coarse rows read received slots. For one k, the entries of one aligned block of 128 coarse rows lie in one aligned block of 128 columns. `coarse_col`: only a device's first 1024 coarse rows read neighbours' rows. For one k, the entries of one aligned block of 128 coarse rows lie in one aligned block of 128 columns. `remote_row`: for one k and one direction, the entries of one aligned block of 128 slots lie in one aligned block of 128 coarse rows. `interp_row`: for one k, the entries of one run of 128 cells along z that starts at a multiple of 128 lie in one aligned block of 128 coarse rows.
All inputs are finite; a program needn't handle non-finite values.
Results may differ from the reference program's by a relative error of at most 0.0003.
Values sent between devices are 32-bit elements; how exact they have to be, the bound alone decides.
A program may use at most 128 MiB of HBM per device.

```python
import jax
import jax.numpy as jnp

CX = 8
CY = 8
NZ = 512
CAP = 4096
BLK = 128
KR = 27
KI = 4
KA = 16
NX = 32
NY = 64
NCD = 4096
NRIM = 1024
N_GX = 4
N_GY = 8
DEVICES = 32


OFFSET_X = (-1, -1, -1, 0, 0, 1, 1, 1)


OFFSET_Y = (-1, 0, 1, -1, 1, -1, 0, 1)


def draw_send_count(key, part):
    key_heavy_x, key_heavy_y, key_busy, key_lower, key_upper = jax.random.split(jax.random.fold_in(key, 7), 5)
    heavy_x = jax.random.randint(key_heavy_x, (), 1, N_GX - 1)
    heavy_y = jax.random.randint(key_heavy_y, (), 1, N_GY - 1)
    is_busy = jax.random.randint(key_busy, (N_GX + 2, N_GY + 2), 0, 4) == 0
    step_x = jnp.array(OFFSET_X, jnp.int32)[None, None, :]
    step_y = jnp.array(OFFSET_Y, jnp.int32)[None, None, :]
    dest_x = jnp.arange(N_GX, dtype=jnp.int32)[:, None, None] + step_x
    dest_y = jnp.arange(N_GY, dtype=jnp.int32)[None, :, None] + step_y
    exists = (dest_x >= 0) & (dest_x < N_GX) & (dest_y >= 0) & (dest_y < N_GY)
    low_counts = jax.random.randint(key_lower, (N_GX, N_GY, 8), max(1, CAP // 6), CAP // 3 + 1)
    high_counts = jax.random.randint(key_upper, (N_GX, N_GY, 8), CAP // 2, CAP + 1)
    counts = jnp.where(is_busy[dest_x + 1, dest_y + 1], high_counts, low_counts)
    counts = jnp.where((dest_x == heavy_x) & (dest_y == heavy_y), CAP, counts)
    counts = jnp.where(exists, counts, 0)
    return counts.astype(jnp.int32)


def draw_send_cell(key, part):
    key_x, key_y, key_z, key_off = jax.random.split(jax.random.fold_in(key, 11), 4)
    step_x = jnp.array(OFFSET_X, jnp.int32)[None, None, :, None]
    step_y = jnp.array(OFFSET_Y, jnp.int32)[None, None, :, None]
    band_width = jnp.where((step_x != 0) & (step_y != 0), 4, 2)
    low_x = jnp.where(step_x == 1, CX - band_width, 0)
    high_x = jnp.where(step_x == -1, band_width, CX)
    low_y = jnp.where(step_y == 1, CY - band_width, 0)
    high_y = jnp.where(step_y == -1, band_width, CY)
    block_shape = (N_GX, N_GY, 8, CAP // BLK)
    cell_x = jax.random.randint(key_x, block_shape, low_x, high_x)
    cell_y = jax.random.randint(key_y, block_shape, low_y, high_y)
    z_block = jax.random.randint(key_z, block_shape, 0, NZ // BLK)
    offset = jax.random.randint(key_off, block_shape + (BLK,), 0, BLK)
    start = (cell_x * CY + cell_y) * NZ + z_block * BLK
    return (start[..., None] + offset).reshape(N_GX, N_GY, 8, CAP).astype(jnp.int32)


def blocked_columns(key, lead_shape, row_blocks, rim_blocks, near_blocks, far_blocks):
    key_far, key_near, key_pick, key_off = jax.random.split(key, 4)
    block_shape = lead_shape + (row_blocks,)
    block_ids = jnp.arange(row_blocks, dtype=jnp.int32)
    is_far = (jax.random.randint(key_far, block_shape, 0, 2) == 1) & (block_ids < rim_blocks)
    near_base = jax.random.randint(key_near, block_shape, 0, near_blocks)
    far_base = near_blocks + jax.random.randint(key_pick, block_shape, 0, far_blocks)
    base = jnp.where(is_far, far_base, near_base)
    offset = jax.random.randint(key_off, block_shape + (BLK,), 0, BLK)
    return (base[..., None] * BLK + offset).reshape(lead_shape + (row_blocks * BLK,)).astype(jnp.int32)


def draw_restrict_col(key, part):
    return blocked_columns(jax.random.fold_in(key, 13), (KR, N_GX, N_GY), NCD // BLK, NRIM // BLK, CX * CY * NZ // BLK, 8 * CAP // BLK)


def draw_coarse_col(key, part):
    return blocked_columns(jax.random.fold_in(key, 17), (KA, N_GX, N_GY), NCD // BLK, NRIM // BLK, NCD // BLK, 8 * NRIM // BLK)


def draw_remote_row(key, part):
    return blocked_columns(jax.random.fold_in(key, 19), (KI, N_GX, N_GY, 8), CAP // BLK, 0, NCD // BLK, 1)


def draw_interp_row(key, part):
    return blocked_columns(jax.random.fold_in(key, 23), (KI, NX, NY), NZ // BLK, 0, NCD // BLK, 1)


def block_scale(own_key, extent, cuts, smallest, high):
    level, own = 1.0, jax.random.fold_in(own_key, 6)
    for position, blocks in cuts:
        draws = jnp.exp(jax.random.uniform(jax.random.fold_in(own, position), (blocks,), jnp.float32, smallest / len(cuts), high / len(cuts)))
        level = level * jnp.repeat(draws, extent[position] // blocks).reshape([-1 if axis == position else 1 for axis in range(len(extent))])
    return level


def centred(own_key, extent, scale, most, cuts=(), kind=jnp.bfloat16):
    loudness = block_scale(own_key, extent, cuts, -0.22, 0.18) if cuts else 1.0
    values = jax.random.normal(own_key, extent, jnp.float32) * scale * loudness
    return jnp.minimum(jnp.maximum(values, -most), most).astype(kind)


def setup_inputs(seed: int = 0) -> dict:
    splits = jax.random.split(jax.random.key(seed), 18)
    return {
        "rhs": centred(splits[0], (NX, NY, NZ), 3.0, 18.0, ((0, 4), (1, 8)), jnp.float32),
        "diag": jnp.clip(0.5 + 1.5 * jax.random.uniform(splits[1], (NX, NY, NZ), jnp.float32) ** block_scale(splits[1], (NX, NY, NZ), ((0, 4), (1, 8)), -0.2, 0.2), 0.5, 2.0),
        "smoother_center": jnp.clip(0.1 + 0.1 * jax.random.uniform(splits[2], (NX, NY, NZ), jnp.float32) ** block_scale(splits[2], (NX, NY, NZ), ((0, 4), (1, 8)), -0.2, 0.2), 0.1, 0.2),
        "smoother_faces": jnp.clip(0.01 + 0.04 * jax.random.uniform(splits[3], (6, NX, NY, NZ), jnp.float32) ** block_scale(splits[3], (6, NX, NY, NZ), ((1, 4), (2, 8)), -0.2, 0.2), 0.01, 0.05),
        "send_count": draw_send_count(jax.random.fold_in(splits[17], 71), 0),
        "send_cell": draw_send_cell(jax.random.fold_in(splits[17], 71), 0),
        "restrict_col": draw_restrict_col(jax.random.fold_in(splits[17], 71), 0),
        "restrict_vals": jnp.clip(0.03 + 0.17 * jax.random.uniform(splits[7], (KR, N_GX, N_GY, NCD), jnp.float32) ** block_scale(splits[7], (KR, N_GX, N_GY, NCD), ((1, 4), (2, 8)), -0.2, 0.2), 0.03, 0.2),
        "coarse_col": draw_coarse_col(jax.random.fold_in(splits[17], 71), 0),
        "coarse_diag": jnp.clip(3.0 + 3.0 * jax.random.uniform(splits[9], (N_GX, N_GY, NCD), jnp.float32) ** block_scale(splits[9], (N_GX, N_GY, NCD), ((0, 4), (1, 8)), -0.2, 0.2), 3.0, 6.0),
        "coarse_vals": centred(splits[10], (KA, N_GX, N_GY, NCD), 0.5, 3.0, ((1, 4), (2, 8)), jnp.float32),
        "csmooth_diag": jnp.clip(0.15 + 0.15 * jax.random.uniform(splits[11], (N_GX, N_GY, NCD), jnp.float32) ** block_scale(splits[11], (N_GX, N_GY, NCD), ((0, 4), (1, 8)), -0.2, 0.2), 0.15, 0.3),
        "csmooth_vals": centred(splits[12], (KA, N_GX, N_GY, NCD), 0.05, 0.3, ((1, 4), (2, 8)), jnp.float32),
        "remote_row": draw_remote_row(jax.random.fold_in(splits[17], 71), 0),
        "remote_vals": jnp.clip(0.3 + 0.7 * jax.random.uniform(splits[14], (KI, N_GX, N_GY, 8, CAP), jnp.float32) ** block_scale(splits[14], (KI, N_GX, N_GY, 8, CAP), ((1, 4), (2, 8)), -0.2, 0.2), 0.3, 1.0),
        "interp_row": draw_interp_row(jax.random.fold_in(splits[17], 71), 0),
        "interp_vals": jnp.clip(0.3 + 0.7 * jax.random.uniform(splits[16], (KI, NX, NY, NZ), jnp.float32) ** block_scale(splits[16], (KI, NX, NY, NZ), ((1, 4), (2, 8)), -0.2, 0.2), 0.3, 1.0),
    }


OFFSETS = ((-1, -1), (-1, 0), (-1, 1), (0, -1), (0, 1), (1, -1), (1, 0), (1, 1))


def fine_neighbours(field):
    padded = jnp.pad(field, 1)
    return [padded[:-2, 1:-1, 1:-1], padded[2:, 1:-1, 1:-1],
            padded[1:-1, :-2, 1:-1], padded[1:-1, 2:, 1:-1],
            padded[1:-1, 1:-1, :-2], padded[1:-1, 1:-1, 2:]]


def apply_operator(field, diag):
    beside = fine_neighbours(field)
    beside_sum = beside[0]
    for which in range(1, 6):
        beside_sum = beside_sum + beside[which]
    return (6.0 + diag) * field - beside_sum


def apply_smoother(field, center, faces):
    beside = fine_neighbours(field)
    result = center * field
    for which in range(6):
        result = result + faces[which] * beside[which]
    return result


def to_blocks(field):
    return field.reshape(N_GX, CX, N_GY, CY, NZ).transpose(0, 2, 1, 3, 4).reshape(DEVICES, CX * CY * NZ)


def from_blocks(flat_cells):
    return flat_cells.reshape(N_GX, N_GY, CX, CY, NZ).transpose(0, 2, 1, 3, 4).reshape(NX, NY, NZ)


def lookup(table, index):
    return jax.vmap(lambda row_table, row_index: row_table[row_index], in_axes=(0, 1), out_axes=1)(table, index)


def from_neighbours(send_grid):
    padded = jnp.pad(send_grid, ((1, 1), (1, 1), (0, 0), (0, 0)))
    pieces = []
    for slot_dir in range(8):
        step_x, step_y = OFFSETS[slot_dir]
        pieces.append(padded[1 + step_x:1 + step_x + N_GX, 1 + step_y:1 + step_y + N_GY, 7 - slot_dir])
    return jnp.stack(pieces, axis=2)


def rim_of(vector):
    padded = jnp.pad(vector[:, :, :NRIM], ((1, 1), (1, 1), (0, 0)))
    pieces = []
    for slot_dir in range(8):
        step_x, step_y = OFFSETS[slot_dir]
        pieces.append(padded[1 + step_x:1 + step_x + N_GX, 1 + step_y:1 + step_y + N_GY])
    return jnp.stack(pieces, axis=2)


def coarse_apply(vector, diagonal, values, column):
    coarse_table = jnp.concatenate([vector, rim_of(vector).reshape(N_GX, N_GY, 8 * NRIM)], axis=2)
    coarse_table = coarse_table.reshape(DEVICES, NCD + 8 * NRIM)
    gathered = lookup(coarse_table, column.astype(jnp.int32).reshape(KA, DEVICES, NCD)).reshape(KA, N_GX, N_GY, NCD)
    return diagonal * vector + jnp.sum(values * gathered, axis=0)


def reference(rhs, diag, smoother_center, smoother_faces, send_count, send_cell, restrict_col,
              restrict_vals, coarse_col, coarse_diag, coarse_vals, csmooth_diag, csmooth_vals,
              remote_row, remote_vals, interp_row, interp_vals):
    cells_dev = CX * CY * NZ
    x_first = apply_smoother(rhs, smoother_center, smoother_faces)
    r_first = rhs - apply_operator(x_first, diag)
    r_blocks = to_blocks(r_first)
    cell_ids = send_cell.astype(jnp.int32).reshape(DEVICES, 8 * CAP)
    slot_ids = jnp.arange(CAP, dtype=jnp.int32)
    is_live = slot_ids[None, None, None, :] < send_count[..., None]
    picked = jnp.take_along_axis(r_blocks, cell_ids, axis=1).reshape(N_GX, N_GY, 8, CAP)
    sent_vals = jnp.where(is_live, picked, jnp.float32(0.0))
    received = from_neighbours(sent_vals).reshape(DEVICES, 8 * CAP)
    fine_table = jnp.concatenate([r_blocks, received], axis=1)
    restrict_index = restrict_col.astype(jnp.int32).reshape(KR, DEVICES, NCD)
    coarse_rhs = jnp.sum(restrict_vals.reshape(KR, DEVICES, NCD) * lookup(fine_table, restrict_index), axis=0)
    coarse_rhs = coarse_rhs.reshape(N_GX, N_GY, NCD)
    coarse_first = coarse_apply(coarse_rhs, csmooth_diag, csmooth_vals, coarse_col)
    coarse_resid = coarse_rhs - coarse_apply(coarse_first, coarse_diag, coarse_vals, coarse_col)
    coarse_second = coarse_first + coarse_apply(coarse_resid, csmooth_diag, csmooth_vals, coarse_col)
    second_flat = coarse_second.reshape(DEVICES, NCD)
    remote_index = remote_row.astype(jnp.int32).reshape(KI, DEVICES, 8 * CAP)
    back_vals = jnp.sum(remote_vals.reshape(KI, DEVICES, 8 * CAP) * lookup(second_flat, remote_index), axis=0)
    back_vals = back_vals.reshape(N_GX, N_GY, 8, CAP)
    returned = jnp.where(is_live, from_neighbours(back_vals), jnp.float32(0.0)).reshape(DEVICES, 8 * CAP)
    interp_index = jnp.stack([to_blocks(interp_row[term]) for term in range(KI)]).astype(jnp.int32)
    interp_weight = jnp.stack([to_blocks(interp_vals[term]) for term in range(KI)])
    local_part = jnp.sum(interp_weight * lookup(second_flat, interp_index), axis=0)
    scattered = jax.vmap(lambda where_to, amount: jnp.zeros((cells_dev,), jnp.float32).at[where_to].add(amount))(cell_ids, returned)
    x_second = x_first + from_blocks(local_part + scattered)
    r_second = rhs - apply_operator(x_second, diag)
    solution = x_second + apply_smoother(r_second, smoother_center, smoother_faces)
    residual = rhs - apply_operator(solution, diag)
    return solution, residual
```

```python
import jax
import jax.numpy as jnp
from jax import lax
from jax.experimental import pallas as pl
from jax.experimental.pallas import tpu as pltpu
from jax.sharding import PartitionSpec as P

BLK = 128
OFFSETS = ((-1, -1), (-1, 0), (-1, 1), (0, -1), (0, 1), (1, -1), (1, 0), (1, 1))
SIDES = ((-1, 0), (1, 0), (0, -1), (0, 1))
CORNERS = (0, 2, 5, 7)
MESH_ID = pl.DeviceIdType.MESH


def split_two(table):
    high = table.astype(jnp.bfloat16)
    low = (table - high.astype(jnp.float32)).astype(jnp.bfloat16)
    return jnp.concatenate([high, low], axis=1)


def one_hot(base, width):
    ids = lax.broadcasted_iota(jnp.int32, (base.shape[0], width), 1)
    return jnp.where(ids == base, 1.0, 0.0).astype(jnp.bfloat16)


def pick(index, base, table_two):
    both = jnp.dot(
        one_hot(base, table_two.shape[0]), table_two, preferred_element_type=jnp.float32
    )
    rows = both[:, :BLK] + both[:, BLK:]
    return jnp.take_along_axis(rows, index & (BLK - 1), axis=1, mode="promise_in_bounds")


def make_kernel(sizes, shapes):
    na, nb = sizes
    cx, cy, nz = shapes["rhs"]
    zblocks = nz // BLK
    cells = cx * cy
    fine_rows = cells * zblocks
    cap = shapes["send_cell"][1]
    slots = cap // BLK
    kr, crows, _ = shapes["restrict_col"]
    ka = shapes["coarse_col"][0]
    ki = shapes["interp_row"][0]
    rim_rows = 8

    def fine_place(block):
        return (block % zblocks) * cells + block // zblocks

    def kernel(
        rhs_h, diag_h, center_h, faces_h, count_ref, cell_h, rcol_h, rval_h, ccol_h,
        cdiag_h, cval_h, mdiag_h, mval_h, rrow_h, rrval_h, irow_h, ival_h,
        sol_ref, res_ref,
        field, yrecv, diag, center, faces, edges, cell, rcol, rval, ccol, cdiag, cval,
        mdiag, mval, rrow, rrval, irow, ival, resid, fine_two, choose, sent, received,
        back, returned, coarse, rim, spread, partial,
        first_out, first_in, pre_out, pre_in, last_out, last_in, tip_out, tip_in, edges_in,
        in_sem, first_send, first_recv, pre_send, pre_recv, last_send, last_recv,
        tip_send, tip_recv, edges_send, edges_recv,
        slot_send, slot_recv, back_send, back_recv, rim_send, rim_recv,
    ):
        a = lax.axis_index("gx")
        b = lax.axis_index("gy")

        loads = [
            (rhs_h, field.at[0, pl.ds(1, cx)]), (center_h, center), (faces_h, faces),
            (center_h.at[0], edges.at[0, 0]), (center_h.at[cx - 1], edges.at[1, 0]),
            (center_h.at[:, 0, :], edges.at[2, 0]), (center_h.at[:, cy - 1, :], edges.at[3, 0]),
            (faces_h.at[:, 0], edges.at[0, pl.ds(1, 6)]),
            (faces_h.at[:, cx - 1], edges.at[1, pl.ds(1, 6)]),
            (faces_h.at[:, :, 0, :], edges.at[2, pl.ds(1, 6)]),
            (faces_h.at[:, :, cy - 1, :], edges.at[3, pl.ds(1, 6)]),
            (diag_h, diag), (cell_h, cell), (rcol_h, rcol), (rval_h, rval),
            (ccol_h, ccol), (mdiag_h, mdiag), (mval_h, mval), (cdiag_h, cdiag),
            (cval_h, cval), (rrow_h, rrow), (rrval_h, rrval), (irow_h, irow),
            (ival_h, ival),
        ]
        loads = [
            pltpu.make_async_copy(source, target, in_sem.at[n])
            for n, (source, target) in enumerate(loads)
        ]
        for load in loads:
            load.start()

        def there(step):
            dx, dy = step
            checks = []
            if dx < 0:
                checks.append(a > 0)
            if dx > 0:
                checks.append(a < na - 1)
            if dy < 0:
                checks.append(b > 0)
            if dy > 0:
                checks.append(b < nb - 1)
            out = checks[0]
            for check in checks[1:]:
                out = jnp.logical_and(out, check)
            return out

        exists = [there(step) for step in OFFSETS]
        side_exists = [there(step) for step in SIDES]

        barrier = pltpu.get_barrier_semaphore()
        total = jnp.int32(0)
        for d, (dx, dy) in enumerate(OFFSETS):
            @pl.when(exists[d])
            def _():
                pl.semaphore_signal(
                    barrier, inc=1, device_id=(a + dx, b + dy), device_id_type=MESH_ID
                )
            total = total + exists[d].astype(jnp.int32)

        for s in range(4):
            @pl.when(jnp.logical_not(side_exists[s]))
            def _():
                first_in[s] = jnp.zeros(first_in.shape[1:], jnp.float32)
                last_in[s] = jnp.zeros(last_in.shape[1:], jnp.float32)
                edges_in[s] = jnp.zeros(edges_in.shape[1:], jnp.float32)
        for c in range(4):
            @pl.when(jnp.logical_not(exists[CORNERS[c]]))
            def _():
                pre_in[c] = jnp.zeros(pre_in.shape[1:], jnp.float32)
                tip_in[c] = jnp.zeros(tip_in.shape[1:], jnp.float32)
        for d in range(8):
            @pl.when(jnp.logical_not(exists[d]))
            def _():
                received[d] = jnp.zeros((slots, BLK), jnp.float32)
                returned[d] = jnp.zeros((slots, BLK), jnp.float32)
                for t in range(3):
                    rim[t, d] = jnp.zeros((rim_rows, BLK), jnp.float32)

        def item(cond, step, src, there_ref, here_ref, send, there_sem, here_sem):
            target = (a + step[0], b + step[1])

            def copy():
                return pltpu.make_async_remote_copy(
                    src_ref=src, dst_ref=there_ref, send_sem=send, recv_sem=there_sem,
                    device_id=target, device_id_type=MESH_ID,
                )

            def arrival():
                return pltpu.make_async_remote_copy(
                    src_ref=here_ref, dst_ref=here_ref, send_sem=send, recv_sem=here_sem,
                    device_id=target, device_id_type=MESH_ID,
                )

            return cond, copy, arrival

        def side_items(out, into, send, recv):
            return [
                item(
                    side_exists[s], SIDES[s], out(s), into(s ^ 1), into(s),
                    send(s), recv(s ^ 1), recv(s),
                )
                for s in (2, 3, 0, 1)
            ]

        def corner_items(out, into, send, recv):
            return [
                item(
                    exists[CORNERS[c]], OFFSETS[CORNERS[c]], out.at[c], into.at[3 - c],
                    into.at[c], send.at[c], recv.at[3 - c], recv.at[c],
                )
                for c in range(4)
            ]

        first_items = corner_items(pre_out, pre_in, pre_send, pre_recv) + side_items(
            lambda s: first_out.at[s], lambda s: first_in.at[s],
            lambda s: first_send.at[s], lambda s: first_recv.at[s],
        )
        last_items = corner_items(tip_out, tip_in, tip_send, tip_recv) + side_items(
            lambda s: last_out.at[s], lambda s: last_in.at[s],
            lambda s: last_send.at[s], lambda s: last_recv.at[s],
        )

        def edge_items(t):
            low, size = ((0, 3), (3, 2), (5, 2))[t]
            return side_items(
                lambda s: edges.at[s, pl.ds(low, size)],
                lambda s: edges_in.at[s, pl.ds(low, size)],
                lambda s: edges_send.at[t, s], lambda s: edges_recv.at[t, s],
            )

        def start_items(items):
            for cond, copy, _ in items:
                @pl.when(cond)
                def _():
                    copy().start()

        def wait_items(items):
            for cond, _, arrival in items:
                @pl.when(cond)
                def _():
                    arrival().wait_recv()

        def finish_items(items):
            for cond, copy, _ in items:
                @pl.when(cond)
                def _():
                    copy().wait_send()

        def eight_copy(src, dst, send_sem, recv_sem, d):
            dx, dy = OFFSETS[d]
            return pltpu.make_async_remote_copy(
                src_ref=src(d), dst_ref=dst(7 - d), send_sem=send_sem(d),
                recv_sem=recv_sem(7 - d),
                device_id=(a + dx, b + dy), device_id_type=MESH_ID,
            )

        def eight_arrival(dst, send_sem, recv_sem, d):
            dx, dy = OFFSETS[d]
            return pltpu.make_async_remote_copy(
                src_ref=dst(d), dst_ref=dst(d), send_sem=send_sem(d), recv_sem=recv_sem(d),
                device_id=(a + dx, b + dy), device_id_type=MESH_ID,
            )

        slot_plan = (
            lambda d: sent.at[d], lambda d: received.at[d],
            lambda d: slot_send.at[d], lambda d: slot_recv.at[d],
        )
        back_plan = (
            lambda d: back.at[d], lambda d: returned.at[d],
            lambda d: back_send.at[d], lambda d: back_recv.at[d],
        )

        def rim_plan(t):
            return (
                lambda d: coarse.at[t, pl.ds(0, rim_rows)], lambda d: rim.at[t, d],
                lambda d: rim_send.at[t, d], lambda d: rim_recv.at[t, d],
            )

        def start_eight(plan):
            for d in (0, 2, 5, 7, 3, 4, 1, 6):
                @pl.when(exists[d])
                def _():
                    eight_copy(*plan, d).start()

        def wait_eight(plan):
            for d in range(8):
                @pl.when(exists[d])
                def _():
                    eight_arrival(*plan[1:], d).wait_recv()

        row_ids = lax.broadcasted_iota(jnp.int32, (cy, nz), 0)
        lane_ids = lax.broadcasted_iota(jnp.int32, (cy, nz), 1)

        zeros = jnp.zeros((cy, nz), jnp.float32)

        def beside(t, i):
            centre = field[t, i + 1]
            return centre, [
                field[t, i] if i > 0 else zeros,
                field[t, i + 2] if i < cx - 1 else zeros,
                jnp.where(row_ids == 0, 0.0, pltpu.roll(centre, 1, 0)),
                jnp.where(row_ids == cy - 1, 0.0, pltpu.roll(centre, cy - 1, 0)),
                jnp.where(lane_ids == 0, 0.0, pltpu.roll(centre, 1, 1)),
                jnp.where(lane_ids == nz - 1, 0.0, pltpu.roll(centre, nz - 1, 1)),
            ]

        def sides(t, i):
            out = [
                jnp.where(row_ids == 0, jnp.broadcast_to(yrecv[t, 0, i:i + 1, :], (cy, nz)), 0.0),
                jnp.where(row_ids == cy - 1, jnp.broadcast_to(yrecv[t, 1, i:i + 1, :], (cy, nz)), 0.0),
            ]
            return [
                field[t, 0] if i == 0 else None,
                field[t, cx + 1] if i == cx - 1 else None,
            ] + out

        def residual_inside(t):
            for i in range(cx):
                centre, near = beside(t, i)
                sums = near[0]
                for one in near[1:]:
                    sums = sums + one
                partial[i] = field[0, i + 1] - ((6.0 + diag[i]) * centre - sums)

        def residual_row(t, i):
            out = partial[i]
            for one in sides(t, i):
                if one is not None:
                    out = out + one
            return out

        def smoother_inside(t, base):
            for i in range(cx):
                centre, near = beside(t, i)
                out = center[i] * centre
                for q in range(6):
                    out = out + faces[q, i] * near[q]
                partial[i] = out if base is None else field[base, i + 1] + out

        def smoother_row(t, i):
            out = partial[i]
            for q, one in enumerate(sides(t, i)):
                if one is not None:
                    out = out + faces[q, i] * one
            return out

        def put_edges(out, n, i, value):
            base = n * zblocks * 8
            for z in range(zblocks):
                part = value[:, z * BLK:(z + 1) * BLK]
                row = base + z * 8
                if i == 0:
                    out[0, row:row + 8, :] = part
                if i == cx - 1:
                    out[1, row:row + 8, :] = part
                out[2, row + i:row + i + 1, :] = part[0:1]
                out[3, row + i:row + i + 1, :] = part[cy - 1:cy]

        def layer(ref, s, n):
            base = n * zblocks * 8
            return jnp.concatenate(
                [ref[s, base + 8 * z:base + 8 * z + 8, :] for z in range(zblocks)], axis=1
            )

        def column(ref, c, low, step=1):
            return jnp.concatenate(
                [ref[c, low + z * step:low + z * step + 1, :] for z in range(zblocks)], axis=1
            )

        def put_column(ref, c, low, value):
            for z in range(zblocks):
                ref[c, low + z:low + z + 1, :] = value[:, z * BLK:(z + 1) * BLK]

        def corner_cell(c):
            dx, dy = OFFSETS[CORNERS[c]]
            return (0 if dx < 0 else cx - 1), (0 if dy < 0 else cy - 1), -dx, -dy

        away = [1 + s for s in range(4)]
        facing = [1 + (s ^ 1) for s in range(4)]
        along = [(3, 4), (3, 4), (1, 2), (1, 2)]
        ends = [(0, 1), (2, 3), (0, 2), (1, 3)]
        first_row, last_row = row_ids == 0, row_ids == cy - 1

        def at_ends(low, high):
            wide = (cy, nz)
            return jnp.where(
                first_row, jnp.broadcast_to(low, wide),
                jnp.where(last_row, jnp.broadcast_to(high, wide), 0.0),
            )

        for load in loads[0:3]:
            load.wait()
        smoother_inside(0, None)
        for i in range(cx):
            put_edges(first_out, 0, i, field[0, i + 1])
            put_edges(first_out, 1, i, partial[i])
        for c in range(4):
            i, j, _, _ = corner_cell(c)
            put_column(pre_out, c, 0, field[0, i + 1][j:j + 1])
        for load in loads[3:11]:
            load.wait()
        end_row = 3 * zblocks * 8
        for s in range(4):
            face = edges[s, 1 + s]
            low, high = along[s]
            at_low, at_high = edges[s, low][0:1], edges[s, high][cy - 1:cy]
            for z in range(zblocks):
                row = 2 * zblocks * 8 + z * 8
                first_out[s, row:row + 8, :] = face[:, z * BLK:(z + 1) * BLK]
                first_out[s, end_row + z:end_row + z + 1, :] = at_low[:, z * BLK:(z + 1) * BLK]
                row = end_row + zblocks + z
                first_out[s, row:row + 1, :] = at_high[:, z * BLK:(z + 1) * BLK]
        pl.semaphore_wait(barrier, total)
        start_items(first_items)
        loads = loads[10:]
        for load in loads[1:3]:
            load.wait()

        cell_index = jnp.concatenate(
            [cell[:, s * BLK:(s + 1) * BLK] for s in range(slots)], axis=0
        )
        cell_base = fine_place(cell_index[:, 0:1] // BLK)
        across = jnp.transpose(
            jnp.broadcast_to(cell_base, (8 * slots, BLK)).astype(jnp.float32)
        )[0:1].astype(jnp.int32)
        fine_ids = lax.broadcasted_iota(jnp.int32, (fine_rows, 8 * slots), 0)
        choose[...] = jnp.where(fine_ids == across, 1.0, 0.0).astype(jnp.bfloat16)

        for load in loads[3:]:
            load.wait()
        wait_items(first_items)

        def set_ghost(t, s, value):
            if s < 2:
                field[t, 0 if s == 0 else cx + 1] = value
            else:
                yrecv[t, s - 2] = value

        for s in range(4):
            set_ghost(0, s, layer(first_in, s, 0))
            low, high = ends[s]
            set_ghost(1, s, (
                layer(first_in, s, 1) + layer(first_in, s, 2) * layer(first_out, s, 0)
                + at_ends(
                    column(first_in, s, end_row) * column(pre_in, low, 0),
                    column(first_in, s, end_row + zblocks) * column(pre_in, high, 0),
                )
            ))
        for i in range(cx):
            field[1, i + 1] = smoother_row(0, i)
        residual_inside(1)
        for i in range(cx):
            resid[i] = residual_row(1, i)
        table = jnp.concatenate(
            [resid[:, :, z * BLK:(z + 1) * BLK].reshape(cells, BLK) for z in range(zblocks)],
            axis=0,
        )
        fine_two[...] = split_two(table)

        picked = pick(cell_index, cell_base, fine_two[...])
        lanes = lax.broadcasted_iota(jnp.int32, (8, BLK), 1)
        for s in range(slots):
            live = lanes + s * BLK < count_ref[...]
            values = jnp.where(live, picked[8 * s:8 * s + 8], 0.0)
            for d in range(8):
                sent[d, s:s + 1, :] = values[d:d + 1]
        start_eight(slot_plan)

        step = 9 if kr % 9 == 0 else 1

        def restrict_some(c, acc):
            index = rcol[pl.ds(c * step, step)].reshape(step * crows, BLK)
            block = index[:, 0:1] // BLK
            base = jnp.where(block < fine_rows, fine_place(block), -1)
            got = pick(index, base, fine_two[...]).reshape(step, crows, BLK)
            return acc + jnp.sum(got * rval[pl.ds(c * step, step)], axis=0)

        rc = lax.fori_loop(
            0, kr // step, restrict_some, jnp.zeros((crows, BLK), jnp.float32)
        )
        wait_eight(slot_plan)
        received_two = split_two(received[...].reshape(8 * slots, BLK))
        index = rcol[:, 0:rim_rows, :].reshape(kr * rim_rows, BLK)
        got = pick(index, index[:, 0:1] // BLK - fine_rows, received_two)
        more = jnp.sum(
            got.reshape(kr, rim_rows, BLK) * rval[:, 0:rim_rows, :], axis=0
        )
        rc = jnp.concatenate([rc[:rim_rows] + more, rc[rim_rows:]], axis=0)

        def coarse_apply(t, vector, diagonal, values):
            coarse[t] = vector
            start_eight(rim_plan(t))
            start_items(edge_items(t))
            index = ccol[...].reshape(ka * crows, BLK)
            got = pick(index, index[:, 0:1] // BLK, split_two(vector))
            own = diagonal[...] * vector + jnp.sum(
                got.reshape(ka, crows, BLK) * values[...], axis=0
            )
            wait_eight(rim_plan(t))
            index = ccol[:, 0:rim_rows, :].reshape(ka * rim_rows, BLK)
            got = pick(
                index, index[:, 0:1] // BLK - crows,
                split_two(rim[t].reshape(8 * rim_rows, BLK)),
            )
            more = jnp.sum(
                got.reshape(ka, rim_rows, BLK) * values[:, 0:rim_rows, :], axis=0
            )
            return jnp.concatenate([own[:rim_rows] + more, own[rim_rows:]], axis=0)

        xc1 = coarse_apply(0, rc, mdiag, mval)
        rc2 = rc - coarse_apply(1, xc1, cdiag, cval)
        xc2 = xc1 + coarse_apply(2, rc2, mdiag, mval)
        coarse_two = split_two(xc2)

        group = 8 if slots % 8 == 0 else 1
        for c in range(slots // group):
            parts = [(c * group + g) * BLK for g in range(group)]
            index = jnp.concatenate(
                [rrow[:, :, p:p + BLK].reshape(ki * 8, BLK) for p in parts], axis=0
            )
            got = pick(index, index[:, 0:1] // BLK, coarse_two)
            for g, p in enumerate(parts):
                mine = got[g * ki * 8:(g + 1) * ki * 8].reshape(ki, 8, BLK)
                values = jnp.sum(mine * rrval[:, :, p:p + BLK], axis=0)
                for d in range(8):
                    back[d, c * group + g:c * group + g + 1, :] = values[d:d + 1]
        start_eight(back_plan)

        for z in range(zblocks):
            p = z * BLK
            index = irow[:, :, :, p:p + BLK].reshape(ki * cells, BLK)
            got = pick(index, index[:, 0:1] // BLK, coarse_two)
            got = got.reshape(ki, cx, cy, BLK) * ival[:, :, :, p:p + BLK]
            field[2, 1:cx + 1, :, p:p + BLK] = (
                field[1, 1:cx + 1, :, p:p + BLK] + jnp.sum(got, axis=0)
            )
        wait_eight(back_plan)

        fold_rows = lax.broadcasted_iota(jnp.int32, (64, BLK), 0)
        fold_lanes = lax.broadcasted_iota(jnp.int32, (64, BLK), 1)
        fold_index = (fold_lanes % 16) * 8 + fold_rows % 8
        fold_keep = fold_lanes // 16 == fold_rows // 8

        def spread_some(s, carry):
            p = pl.multiple_of(s * BLK, BLK)
            values = jnp.concatenate(
                [returned[d, pl.ds(s, 1), :] for d in range(8)], axis=0
            )
            values = jnp.where(lanes + p < count_ref[...], values, 0.0)
            within = cell[:, pl.ds(p, BLK)] & (BLK - 1)
            upper, lower = within // 16, within % 16
            coarse_part = jnp.concatenate(
                [jnp.where(upper == h, values, 0.0) for h in range(8)], axis=0
            )
            high = coarse_part.astype(jnp.bfloat16)
            low = (coarse_part - high.astype(jnp.float32)).astype(jnp.bfloat16)
            fine_part = jnp.concatenate(
                [jnp.where(lower == l, 1.0, 0.0) for l in range(16)], axis=0
            ).astype(jnp.bfloat16)
            out = lax.dot_general(
                jnp.concatenate([high, low], axis=0), fine_part,
                (((1,), (1,)), ((), ())), preferred_element_type=jnp.float32,
            )
            out = jnp.take_along_axis(
                out[:64] + out[64:], fold_index, axis=1, mode="promise_in_bounds"
            )
            out = jnp.where(fold_keep, out, 0.0).reshape(8, 8, BLK)
            spread[pl.ds(pl.multiple_of(s * 8, 8), 8)] = jnp.sum(out, axis=0)
            return carry

        lax.fori_loop(0, slots, spread_some, 0, unroll=32)
        both = jnp.dot(
            choose[...], split_two(spread[...]), preferred_element_type=jnp.float32
        )
        added = both[:, :BLK] + both[:, BLK:]
        for z in range(zblocks):
            p = z * BLK
            field[2, 1:cx + 1, :, p:p + BLK] = (
                field[2, 1:cx + 1, :, p:p + BLK]
                + added[z * cells:(z + 1) * cells].reshape(cx, cy, BLK)
            )
        residual_inside(2)
        for i in range(cx):
            field[3, i + 1] = partial[i]
        smoother_inside(3, 2)
        for i in range(cx):
            put_edges(last_out, 0, i, field[2, i + 1])
            put_edges(last_out, 1, i, field[3, i + 1])
            put_edges(last_out, 2, i, partial[i])
        for c in range(4):
            i, j, di, dj = corner_cell(c)
            put_column(tip_out, c, 0, field[2, i + 1][j:j + 1])
            put_column(tip_out, c, zblocks, field[2, i + 1][j + dj:j + dj + 1])
            put_column(tip_out, c, 2 * zblocks, field[2, i + 1 + di][j:j + 1])
            put_column(tip_out, c, 3 * zblocks, field[3, i + 1][j:j + 1])
        start_items(last_items)
        for t in range(3):
            wait_items(edge_items(t))
        wait_items(last_items)

        beyond = [layer(last_in, s, 0) for s in range(4)]
        for s in range(4):
            set_ghost(2, s, beyond[s])
        corner_resid = []
        for c in range(4):
            i, j, _, _ = corner_cell(c)
            sx, sy = (0 if i == 0 else 1), (2 if j == 0 else 3)
            value = (
                column(tip_in, c, 3 * zblocks) + beyond[sx][j:j + 1] + beyond[sy][i:i + 1]
            )
            corner_resid.append(jnp.where(exists[CORNERS[c]], value, 0.0))

        for s in range(4):
            low, high = ends[s]
            low_face, high_face = along[s]
            place = 0 if s % 2 == 0 else cy - 1
            low_side, high_side = (2, 3) if s < 2 else (0, 1)
            change = layer(last_out, s, 0) + at_ends(
                column(tip_in, low, 0), column(tip_in, high, 0)
            )
            beyond_resid = jnp.where(
                side_exists[s], layer(last_in, s, 1) + change, 0.0
            )
            set_ghost(3, s, beyond_resid)
            own_resid = layer(last_out, s, 1) + beyond[s] + at_ends(
                beyond[low_side][place:place + 1], beyond[high_side][place:place + 1]
            )
            wide = (cy, nz)
            before = jnp.where(
                first_row, jnp.broadcast_to(corner_resid[low], wide), pltpu.roll(change, 1, 0)
            )
            after = jnp.where(
                last_row, jnp.broadcast_to(corner_resid[high], wide),
                pltpu.roll(change, cy - 1, 0),
            )
            column_low = zblocks if s >= 2 else 2 * zblocks
            second = at_ends(
                column(tip_in, low, column_low), column(tip_in, high, column_low)
            )
            set_ghost(4, s, (
                layer(last_in, s, 2)
                + edges_in[s, 0] * change
                + edges_in[s, low_face] * before
                + edges_in[s, high_face] * after
                + edges_in[s, facing[s]] * own_resid
                + edges_in[s, away[s]] * second
                + edges_in[s, 5] * jnp.where(lane_ids == 0, 0.0, pltpu.roll(change, 1, 1))
                + edges_in[s, 6] * jnp.where(lane_ids == nz - 1, 0.0, pltpu.roll(change, nz - 1, 1))
            ))
        for i in range(cx):
            partial[i] = field[3, i + 1]
        for i in range(cx):
            field[3, i + 1] = residual_row(2, i)
        smoother_inside(3, 2)
        for i in range(cx):
            value = smoother_row(3, i)
            field[4, i + 1] = value
            sol_ref[i] = value
        residual_inside(4)
        for i in range(cx):
            res_ref[i] = residual_row(4, i)

        finish_items(first_items)
        finish_items(last_items)
        for t in range(3):
            finish_items(edge_items(t))
        for plan in (slot_plan, back_plan, rim_plan(0), rim_plan(1), rim_plan(2)):
            for d in range(8):
                @pl.when(exists[d])
                def _():
                    eight_copy(*plan, d).wait_send()

    f32, i32, bf16 = jnp.float32, jnp.int32, jnp.bfloat16
    vm = pltpu.VMEM
    dma = pltpu.SemaphoreType.DMA
    scratch = [
        vm((5, cx + 2, cy, nz), f32), vm((5, 2, cx, nz), f32),
        vm((cx, cy, nz), f32), vm((cx, cy, nz), f32), vm((6, cx, cy, nz), f32),
        vm((4, 7, 8, nz), f32),
        vm((8, cap), i32), vm((kr, crows, BLK), i32), vm((kr, crows, BLK), f32),
        vm((ka, crows, BLK), i32), vm((crows, BLK), f32), vm((ka, crows, BLK), f32),
        vm((crows, BLK), f32), vm((ka, crows, BLK), f32),
        vm((ki, 8, cap), i32), vm((ki, 8, cap), f32),
        vm((ki, cx, cy, nz), i32), vm((ki, cx, cy, nz), f32),
        vm((cx, cy, nz), f32), vm((fine_rows, 2 * BLK), bf16),
        vm((fine_rows, 8 * slots), bf16),
        vm((8, slots, BLK), f32), vm((8, slots, BLK), f32),
        vm((8, slots, BLK), f32), vm((8, slots, BLK), f32),
        vm((3, crows, BLK), f32), vm((3, 8, rim_rows, BLK), f32),
        vm((8 * slots, BLK), f32), vm((cx, cy, nz), f32),
        vm((4, (3 * 8 + 2) * zblocks, BLK), f32), vm((4, (3 * 8 + 2) * zblocks, BLK), f32),
        vm((4, zblocks, BLK), f32), vm((4, zblocks, BLK), f32),
        vm((4, 3 * 8 * zblocks, BLK), f32), vm((4, 3 * 8 * zblocks, BLK), f32),
        vm((4, 4 * zblocks, BLK), f32), vm((4, 4 * zblocks, BLK), f32),
        vm((4, 7, 8, nz), f32),
        dma((24,)), dma((4,)), dma((4,)), dma((4,)), dma((4,)), dma((4,)), dma((4,)),
        dma((4,)), dma((4,)), dma((3, 4)), dma((3, 4)),
        dma((8,)), dma((8,)), dma((8,)), dma((8,)),
        dma((3, 8)), dma((3, 8)),
    ]
    whole = pl.BlockSpec(memory_space=pltpu.VMEM)
    in_hbm = pl.BlockSpec(memory_space=pltpu.HBM)
    return pl.pallas_call(
        kernel,
        out_shape=(
            jax.ShapeDtypeStruct((cx, cy, nz), f32),
            jax.ShapeDtypeStruct((cx, cy, nz), f32),
        ),
        in_specs=[in_hbm] * 4 + [whole] + [in_hbm] * 12,
        out_specs=(whole, whole),
        scratch_shapes=scratch,
        compiler_params=pltpu.CompilerParams(
            collective_id=0, has_side_effects=True, vmem_limit_bytes=40 * 1024 * 1024
        ),
        name="vcycle",
    )


def body(
    rhs, diag, smoother_center, smoother_faces, send_count, send_cell, restrict_col,
    restrict_vals, coarse_col, coarse_diag, coarse_vals, csmooth_diag, csmooth_vals,
    remote_row, remote_vals, interp_row, interp_vals,
):
    def rows(array):
        return array.reshape(array.shape[0], -1, BLK)

    cap = send_cell.shape[-1]
    ki = remote_row.shape[0]
    def in_hbm(array):
        return pltpu.with_memory_space_constraint(array, pltpu.HBM)

    operands = (
        rhs, diag, smoother_center, smoother_faces,
        jnp.broadcast_to(send_count.reshape(8, 1), (8, BLK)),
        send_cell.reshape(8, cap), rows(restrict_col), rows(restrict_vals),
        rows(coarse_col), coarse_diag.reshape(-1, BLK), rows(coarse_vals),
        csmooth_diag.reshape(-1, BLK), rows(csmooth_vals),
        remote_row.reshape(ki, 8, cap), remote_vals.reshape(ki, 8, cap),
        interp_row, interp_vals,
    )
    shapes = {
        "rhs": rhs.shape, "send_cell": (8, cap), "restrict_col": operands[6].shape,
        "coarse_col": operands[8].shape, "interp_row": interp_row.shape,
    }
    sizes = (lax.axis_size("gx"), lax.axis_size("gy"))
    operands = [x if n == 4 else in_hbm(x) for n, x in enumerate(operands)]
    return make_kernel(sizes, shapes)(*operands)


def solution(mesh):
    fine = P("gx", "gy", None)
    listed = P(None, "gx", "gy", None)
    placed = (
        fine, fine, fine, listed, fine, P("gx", "gy", None, None), listed, listed,
        listed, fine, listed, fine, listed,
        P(None, "gx", "gy", None, None), P(None, "gx", "gy", None, None),
        listed, listed,
    )
    return jax.shard_map(
        body, mesh=mesh, in_specs=placed, out_specs=(fine, fine), check_vma=False
    )
```

```python
import jax
import jax.numpy as jnp
from jax import lax
from jax.experimental import pallas as pl
from jax.experimental.pallas import tpu as pltpu
from jax.sharding import PartitionSpec as P

BLK = 128
OFFSETS = ((-1, -1), (-1, 0), (-1, 1), (0, -1), (0, 1), (1, -1), (1, 0), (1, 1))
SIDES = ((-1, 0), (1, 0), (0, -1), (0, 1))
CORNERS = (0, 2, 5, 7)
MESH_ID = pl.DeviceIdType.MESH


def split_two(table):
    high = table.astype(jnp.bfloat16)
    low = (table - high.astype(jnp.float32)).astype(jnp.bfloat16)
    return jnp.concatenate([high, low], axis=1)


def one_hot(base, width):
    ids = lax.broadcasted_iota(jnp.int32, (base.shape[0], width), 1)
    return jnp.where(ids == base, 1.0, 0.0).astype(jnp.bfloat16)


def pick(index, base, table_two):
    return pick_hot(index, one_hot(base, table_two.shape[0]), table_two)


def pick_hot(index, hot, table_two):
    both = jnp.dot(hot, table_two, preferred_element_type=jnp.float32)
    rows = both[:, :BLK] + both[:, BLK:]
    return jnp.take_along_axis(rows, index & (BLK - 1), axis=1, mode="promise_in_bounds")


def make_kernel(sizes, shapes):
    na, nb = sizes
    cx, cy, nz = shapes["rhs"]
    zblocks = nz // BLK
    cells = cx * cy
    fine_rows = cells * zblocks
    cap = shapes["send_cell"][1]
    slots = cap // BLK
    kr, crows, _ = shapes["restrict_col"]
    ka = shapes["coarse_col"][0]
    ki = shapes["interp_row"][0]
    rim_rows = 8

    def fine_place(block):
        return (block % zblocks) * cells + block // zblocks

    def kernel(
        rhs_h, diag_h, center_h, faces_h, count_h, cell_h, rcol_h, rval_h, ccol_h,
        cdiag_h, cval_h, mdiag_h, mval_h, rrow_h, rrval_h, irow_h, ival_h,
        sol_ref, res_ref,
        hot_back, hot_spread, count, counts, field, yrecv, diag, center, faces, edges, cell, rcol, rval, ccol, cdiag, cval,
        mdiag, mval, rrow, rrval, irow, ival, resid, fine_two, choose, sent, received,
        back, returned, coarse, rim, spread, partial,
        first_out, first_in, pre_out, pre_in, last_out, last_in, tip_out, tip_in, edges_in,
        in_sem, first_send, first_recv, pre_send, pre_recv, last_send, last_recv,
        tip_send, tip_recv, edges_send, edges_recv,
        slot_send, slot_recv, back_send, back_recv, rim_send, rim_recv,
    ):
        a = lax.axis_index("gx")
        b = lax.axis_index("gy")

        loads = [
            (rhs_h, field.at[0, pl.ds(1, cx)]), (center_h, center), (faces_h, faces),
            (center_h.at[0], edges.at[0, 0]), (center_h.at[cx - 1], edges.at[1, 0]),
            (center_h.at[:, 0, :], edges.at[2, 0]), (center_h.at[:, cy - 1, :], edges.at[3, 0]),
            (faces_h.at[:, 0], edges.at[0, pl.ds(1, 6)]),
            (faces_h.at[:, cx - 1], edges.at[1, pl.ds(1, 6)]),
            (faces_h.at[:, :, 0, :], edges.at[2, pl.ds(1, 6)]),
            (faces_h.at[:, :, cy - 1, :], edges.at[3, pl.ds(1, 6)]),
            (diag_h, diag), (cell_h, cell), (count_h, count), (rcol_h, rcol), (rval_h, rval),
            (ccol_h, ccol), (mdiag_h, mdiag), (mval_h, mval), (cdiag_h, cdiag),
            (cval_h, cval), (rrow_h, rrow), (rrval_h, rrval), (irow_h, irow),
            (ival_h, ival),
        ]
        loads = [
            pltpu.make_async_copy(source, target, in_sem.at[n])
            for n, (source, target) in enumerate(loads)
        ]

        def there(step):
            dx, dy = step
            checks = []
            if dx < 0:
                checks.append(a > 0)
            if dx > 0:
                checks.append(a < na - 1)
            if dy < 0:
                checks.append(b > 0)
            if dy > 0:
                checks.append(b < nb - 1)
            out = checks[0]
            for check in checks[1:]:
                out = jnp.logical_and(out, check)
            return out

        exists = [there(step) for step in OFFSETS]
        side_exists = [there(step) for step in SIDES]

        barrier = pltpu.get_barrier_semaphore()
        total = jnp.int32(0)
        for d, (dx, dy) in enumerate(OFFSETS):
            @pl.when(exists[d])
            def _():
                pl.semaphore_signal(
                    barrier, inc=1, device_id=(a + dx, b + dy), device_id_type=MESH_ID
                )
            total = total + exists[d].astype(jnp.int32)

        for load in loads[:3]:
            load.start()

        def item(cond, step, src, there_ref, here_ref, send, there_sem, here_sem):
            target = (a + step[0], b + step[1])

            def copy():
                return pltpu.make_async_remote_copy(
                    src_ref=src, dst_ref=there_ref, send_sem=send, recv_sem=there_sem,
                    device_id=target, device_id_type=MESH_ID,
                )

            def arrival():
                return pltpu.make_async_remote_copy(
                    src_ref=here_ref, dst_ref=here_ref, send_sem=send, recv_sem=here_sem,
                    device_id=target, device_id_type=MESH_ID,
                )

            return cond, copy, arrival

        def side_items(out, into, send, recv):
            return [
                item(
                    side_exists[s], SIDES[s], out(s), into(s ^ 1), into(s),
                    send(s), recv(s ^ 1), recv(s),
                )
                for s in (2, 3, 0, 1)
            ]

        def corner_items(out, into, send, recv):
            return [
                item(
                    exists[CORNERS[c]], OFFSETS[CORNERS[c]], out.at[c], into.at[3 - c],
                    into.at[c], send.at[c], recv.at[3 - c], recv.at[c],
                )
                for c in range(4)
            ]

        first_items = corner_items(pre_out, pre_in, pre_send, pre_recv) + side_items(
            lambda s: first_out.at[s], lambda s: first_in.at[s],
            lambda s: first_send.at[s], lambda s: first_recv.at[s],
        )
        part = 8 * zblocks
        early_items = side_items(
            lambda s: last_out.at[s, pl.ds(0, part)], lambda s: last_in.at[s, pl.ds(0, part)],
            lambda s: last_send.at[0, s], lambda s: last_recv.at[0, s],
        )
        last_items = corner_items(tip_out, tip_in, tip_send, tip_recv) + side_items(
            lambda s: last_out.at[s, pl.ds(part, 2 * part)],
            lambda s: last_in.at[s, pl.ds(part, 2 * part)],
            lambda s: last_send.at[1, s], lambda s: last_recv.at[1, s],
        )

        def edge_items(t):
            low, size = ((0, 3), (3, 2), (5, 2))[t]
            return side_items(
                lambda s: edges.at[s, pl.ds(low, size)],
                lambda s: edges_in.at[s, pl.ds(low, size)],
                lambda s: edges_send.at[t, s], lambda s: edges_recv.at[t, s],
            )

        def start_items(items):
            for cond, copy, _ in items:
                @pl.when(cond)
                def _():
                    copy().start()

        def wait_items(items):
            for cond, _, arrival in items:
                @pl.when(cond)
                def _():
                    arrival().wait_recv()

        def finish_items(items):
            for cond, copy, _ in items:
                @pl.when(cond)
                def _():
                    copy().wait_send()

        def eight_copy(src, dst, send_sem, recv_sem, d):
            dx, dy = OFFSETS[d]
            return pltpu.make_async_remote_copy(
                src_ref=src(d), dst_ref=dst(7 - d), send_sem=send_sem(d),
                recv_sem=recv_sem(7 - d),
                device_id=(a + dx, b + dy), device_id_type=MESH_ID,
            )

        def eight_arrival(dst, send_sem, recv_sem, d):
            dx, dy = OFFSETS[d]
            return pltpu.make_async_remote_copy(
                src_ref=dst(d), dst_ref=dst(d), send_sem=send_sem(d), recv_sem=recv_sem(d),
                device_id=(a + dx, b + dy), device_id_type=MESH_ID,
            )

        slot_plan = (
            lambda d: sent.at[d], lambda d: received.at[d],
            lambda d: slot_send.at[d], lambda d: slot_recv.at[d],
        )
        back_plan = (
            lambda d: back.at[d], lambda d: returned.at[d],
            lambda d: back_send.at[d], lambda d: back_recv.at[d],
        )

        def rim_plan(t):
            return (
                lambda d: coarse.at[t, pl.ds(0, rim_rows)], lambda d: rim.at[t, d],
                lambda d: rim_send.at[t, d], lambda d: rim_recv.at[t, d],
            )

        def start_eight(plan):
            for d in (0, 2, 5, 7, 3, 4, 1, 6):
                @pl.when(exists[d])
                def _():
                    eight_copy(*plan, d).start()

        def wait_eight(plan):
            for d in range(8):
                @pl.when(exists[d])
                def _():
                    eight_arrival(*plan[1:], d).wait_recv()

        row_ids = lax.broadcasted_iota(jnp.int32, (cy, nz), 0)
        lane_ids = lax.broadcasted_iota(jnp.int32, (cy, nz), 1)

        zeros = jnp.zeros((cy, nz), jnp.float32)

        def beside(t, i):
            centre = field[t, i + 1]
            return centre, [
                field[t, i] if i > 0 else zeros,
                field[t, i + 2] if i < cx - 1 else zeros,
                jnp.where(row_ids == 0, 0.0, pltpu.roll(centre, 1, 0)),
                jnp.where(row_ids == cy - 1, 0.0, pltpu.roll(centre, cy - 1, 0)),
                jnp.where(lane_ids == 0, 0.0, pltpu.roll(centre, 1, 1)),
                jnp.where(lane_ids == nz - 1, 0.0, pltpu.roll(centre, nz - 1, 1)),
            ]

        def sides(t, i):
            out = [
                jnp.where(row_ids == 0, jnp.broadcast_to(yrecv[t, 0, i:i + 1, :], (cy, nz)), 0.0),
                jnp.where(row_ids == cy - 1, jnp.broadcast_to(yrecv[t, 1, i:i + 1, :], (cy, nz)), 0.0),
            ]
            return [
                field[t, 0] if i == 0 else None,
                field[t, cx + 1] if i == cx - 1 else None,
            ] + out

        def residual_inside(t):
            for i in range(cx):
                centre, near = beside(t, i)
                sums = near[0]
                for one in near[1:]:
                    sums = sums + one
                partial[i] = field[0, i + 1] - ((6.0 + diag[i]) * centre - sums)

        def residual_row(t, i):
            out = partial[i]
            for one in sides(t, i):
                if one is not None:
                    out = out + one
            return out

        def smoother_inside(t, base):
            for i in range(cx):
                centre, near = beside(t, i)
                out = center[i] * centre
                for q in range(6):
                    out = out + faces[q, i] * near[q]
                partial[i] = out if base is None else field[base, i + 1] + out

        def smoother_row(t, i):
            out = partial[i]
            for q, one in enumerate(sides(t, i)):
                if one is not None:
                    out = out + faces[q, i] * one
            return out

        def put_edges(out, n, i, value):
            base = n * zblocks * 8
            for z in range(zblocks):
                part = value[:, z * BLK:(z + 1) * BLK]
                row = base + z * 8
                if i == 0:
                    out[0, row:row + 8, :] = part
                if i == cx - 1:
                    out[1, row:row + 8, :] = part
                out[2, row + i:row + i + 1, :] = part[0:1]
                out[3, row + i:row + i + 1, :] = part[cy - 1:cy]

        def layer(ref, s, n):
            base = n * zblocks * 8
            return jnp.concatenate(
                [ref[s, base + 8 * z:base + 8 * z + 8, :] for z in range(zblocks)], axis=1
            )

        def column(ref, c, low, step=1):
            return jnp.concatenate(
                [ref[c, low + z * step:low + z * step + 1, :] for z in range(zblocks)], axis=1
            )

        def put_column(ref, c, low, value):
            for z in range(zblocks):
                ref[c, low + z:low + z + 1, :] = value[:, z * BLK:(z + 1) * BLK]

        def corner_cell(c):
            dx, dy = OFFSETS[CORNERS[c]]
            return (0 if dx < 0 else cx - 1), (0 if dy < 0 else cy - 1), -dx, -dy

        away = [1 + s for s in range(4)]
        facing = [1 + (s ^ 1) for s in range(4)]
        along = [(3, 4), (3, 4), (1, 2), (1, 2)]
        ends = [(0, 1), (2, 3), (0, 2), (1, 3)]
        first_row, last_row = row_ids == 0, row_ids == cy - 1

        def at_ends(low, high):
            wide = (cy, nz)
            return jnp.where(
                first_row, jnp.broadcast_to(low, wide),
                jnp.where(last_row, jnp.broadcast_to(high, wide), 0.0),
            )

        for load in loads[0:3]:
            load.wait()
        smoother_inside(0, None)
        for i in range(cx):
            put_edges(first_out, 0, i, field[0, i + 1])
            put_edges(first_out, 1, i, partial[i])
        for c in range(4):
            i, j, _, _ = corner_cell(c)
            put_column(pre_out, c, 0, field[0, i + 1][j:j + 1])
        end_row = 3 * zblocks * 8
        face_rows = 2 * zblocks * 8
        for z in range(zblocks):
            p = z * BLK
            row = face_rows + z * 8
            first_out[0, row:row + 8, :] = faces[0, 0, :, p:p + BLK]
            first_out[1, row:row + 8, :] = faces[1, cx - 1, :, p:p + BLK]
            for i in range(cx):
                first_out[2, row + i:row + i + 1, :] = faces[2, i, 0:1, p:p + BLK]
                first_out[3, row + i:row + i + 1, :] = faces[3, i, cy - 1:cy, p:p + BLK]
            for s in range(4):
                place = (0 if s % 2 == 0 else (cx if s < 2 else cy) - 1)
                if s < 2:
                    at_low = faces[2, place, 0:1, p:p + BLK]
                    at_high = faces[3, place, cy - 1:cy, p:p + BLK]
                else:
                    at_low = faces[0, 0, place:place + 1, p:p + BLK]
                    at_high = faces[1, cx - 1, place:place + 1, p:p + BLK]
                first_out[s, end_row + z:end_row + z + 1, :] = at_low
                row_high = end_row + zblocks + z
                first_out[s, row_high:row_high + 1, :] = at_high
        pl.semaphore_wait(barrier, total)
        start_items(first_items)
        for load in loads[3:]:
            load.start()
        for s in range(4):
            @pl.when(jnp.logical_not(side_exists[s]))
            def _():
                first_in[s] = jnp.zeros(first_in.shape[1:], jnp.float32)
                last_in[s] = jnp.zeros(last_in.shape[1:], jnp.float32)
                edges_in[s] = jnp.zeros(edges_in.shape[1:], jnp.float32)
        for c in range(4):
            @pl.when(jnp.logical_not(exists[CORNERS[c]]))
            def _():
                pre_in[c] = jnp.zeros(pre_in.shape[1:], jnp.float32)
                tip_in[c] = jnp.zeros(tip_in.shape[1:], jnp.float32)
        for d in range(8):
            @pl.when(jnp.logical_not(exists[d]))
            def _():
                received[d] = jnp.zeros((slots, BLK), jnp.float32)
                returned[d] = jnp.zeros((slots, BLK), jnp.float32)
                for t in range(3):
                    rim[t, d] = jnp.zeros((rim_rows, BLK), jnp.float32)

        edge_loads, loads = loads[3:11], loads[10:]
        for load in loads[1:4]:
            load.wait()
        slot_rows = lax.broadcasted_iota(jnp.int32, (8, BLK), 0)
        value = jnp.zeros((8, BLK), jnp.int32)
        for d in range(8):
            value = jnp.where(slot_rows == d, count[0, 0, d], value)
        counts[...] = value

        cell_index = jnp.concatenate(
            [cell[:, s * BLK:(s + 1) * BLK] for s in range(slots)], axis=0
        )
        cell_base = fine_place(cell_index[:, 0:1] // BLK)
        across = jnp.transpose(
            jnp.broadcast_to(cell_base, (8 * slots, BLK)).astype(jnp.float32)
        )[0:1].astype(jnp.int32)
        fine_ids = lax.broadcasted_iota(jnp.int32, (fine_rows, 8 * slots), 0)
        choose[...] = jnp.where(fine_ids == across, 1.0, 0.0).astype(jnp.bfloat16)
        hot_slot = one_hot(cell_base, fine_rows)

        for load in loads[4:] + edge_loads:
            load.wait()
        group = 8 if slots % 8 == 0 else 1
        batch = group * ki * 8

        def back_index(c):
            parts = [(c * group + g) * BLK for g in range(group)]
            return jnp.concatenate(
                [rrow[:, :, p:p + BLK].reshape(ki * 8, BLK) for p in parts], axis=0
            )

        for c in range(slots // group):
            hot_back[c * batch:(c + 1) * batch] = one_hot(back_index(c)[:, 0:1] // BLK, crows)

        def scatter_some(s, carry):
            lower = cell[:, pl.ds(pl.multiple_of(s * BLK, BLK), BLK)] & 31
            hot_spread[s] = jnp.concatenate(
                [jnp.where(lower == l, 1.0, 0.0) for l in range(32)], axis=0
            ).astype(jnp.bfloat16)
            return carry

        lax.fori_loop(0, slots, scatter_some, 0, unroll=4)
        wait_items(first_items)

        def set_ghost(t, s, value):
            if s < 2:
                field[t, 0 if s == 0 else cx + 1] = value
            else:
                yrecv[t, s - 2] = value

        for s in range(4):
            set_ghost(0, s, layer(first_in, s, 0))
            low, high = ends[s]
            set_ghost(1, s, (
                layer(first_in, s, 1) + layer(first_in, s, 2) * layer(first_out, s, 0)
                + at_ends(
                    column(first_in, s, end_row) * column(pre_in, low, 0),
                    column(first_in, s, end_row + zblocks) * column(pre_in, high, 0),
                )
            ))
        for i in range(cx):
            field[1, i + 1] = smoother_row(0, i)
        residual_inside(1)
        for i in range(cx):
            resid[i] = residual_row(1, i)
        table = jnp.concatenate(
            [resid[:, :, z * BLK:(z + 1) * BLK].reshape(cells, BLK) for z in range(zblocks)],
            axis=0,
        )
        fine_two[...] = split_two(table)

        picked = pick_hot(cell_index, hot_slot, fine_two[...])
        lanes = lax.broadcasted_iota(jnp.int32, (8, BLK), 1)
        for s in range(slots):
            live = lanes + s * BLK < counts[...]
            values = jnp.where(live, picked[8 * s:8 * s + 8], 0.0)
            for d in range(8):
                sent[d, s:s + 1, :] = values[d:d + 1]
        start_eight(slot_plan)

        step = 9 if kr % 9 == 0 else 1

        def restrict_some(c, acc):
            index = rcol[pl.ds(c * step, step)].reshape(step * crows, BLK)
            block = index[:, 0:1] // BLK
            base = jnp.where(block < fine_rows, fine_place(block), -1)
            got = pick(index, base, fine_two[...]).reshape(step, crows, BLK)
            return acc + jnp.sum(got * rval[pl.ds(c * step, step)], axis=0)

        rc = lax.fori_loop(
            0, kr // step, restrict_some, jnp.zeros((crows, BLK), jnp.float32)
        )
        far_index = rcol[:, 0:rim_rows, :].reshape(kr * rim_rows, BLK)
        hot_far = one_hot(far_index[:, 0:1] // BLK - fine_rows, 8 * slots)
        own_index = ccol[...].reshape(ka * crows, BLK)
        hot_own = one_hot(own_index[:, 0:1] // BLK, crows)
        rim_index = ccol[:, 0:rim_rows, :].reshape(ka * rim_rows, BLK)
        hot_rim = one_hot(rim_index[:, 0:1] // BLK - crows, 8 * rim_rows)
        wait_eight(slot_plan)
        received_two = split_two(received[...].reshape(8 * slots, BLK))
        got = pick_hot(far_index, hot_far, received_two)
        more = jnp.sum(
            got.reshape(kr, rim_rows, BLK) * rval[:, 0:rim_rows, :], axis=0
        )
        rc = jnp.concatenate([rc[:rim_rows] + more, rc[rim_rows:]], axis=0)

        def coarse_apply(t, vector, diagonal, values):
            coarse[t] = vector
            start_eight(rim_plan(t))
            if t > 0:
                start_items(edge_items(t - 1))
            got = pick_hot(own_index, hot_own, split_two(vector))
            own = diagonal[...] * vector + jnp.sum(
                got.reshape(ka, crows, BLK) * values[...], axis=0
            )
            wait_eight(rim_plan(t))
            got = pick_hot(
                rim_index, hot_rim, split_two(rim[t].reshape(8 * rim_rows, BLK))
            )
            more = jnp.sum(
                got.reshape(ka, rim_rows, BLK) * values[:, 0:rim_rows, :], axis=0
            )
            return jnp.concatenate([own[:rim_rows] + more, own[rim_rows:]], axis=0)

        xc1 = coarse_apply(0, rc, mdiag, mval)
        rc2 = rc - coarse_apply(1, xc1, cdiag, cval)
        xc2 = xc1 + coarse_apply(2, rc2, mdiag, mval)
        coarse_two = split_two(xc2)

        for c in range(slots // group):
            parts = [(c * group + g) * BLK for g in range(group)]
            got = pick_hot(
                back_index(c), hot_back[c * batch:(c + 1) * batch], coarse_two
            )
            for g, p in enumerate(parts):
                mine = got[g * ki * 8:(g + 1) * ki * 8].reshape(ki, 8, BLK)
                values = jnp.sum(mine * rrval[:, :, p:p + BLK], axis=0)
                for d in range(8):
                    back[d, c * group + g:c * group + g + 1, :] = values[d:d + 1]
        start_eight(back_plan)
        start_items(edge_items(2))

        for z in range(zblocks):
            p = z * BLK
            index = irow[:, :, :, p:p + BLK].reshape(ki * cells, BLK)
            got = pick(index, index[:, 0:1] // BLK, coarse_two)
            got = got.reshape(ki, cx, cy, BLK) * ival[:, :, :, p:p + BLK]
            field[2, 1:cx + 1, :, p:p + BLK] = (
                field[1, 1:cx + 1, :, p:p + BLK] + jnp.sum(got, axis=0)
            )
        wait_eight(back_plan)

        fold_rows = lax.broadcasted_iota(jnp.int32, (32, BLK), 0)
        fold_lanes = lax.broadcasted_iota(jnp.int32, (32, BLK), 1)
        fold_index = (fold_lanes % 16) * 8 + fold_rows % 8
        fold_left = jnp.logical_and(fold_lanes // 32 == fold_rows // 8, fold_lanes % 32 < 16)
        fold_right = jnp.logical_and(fold_lanes // 32 == fold_rows // 8, fold_lanes % 32 >= 16)

        def spread_some(s, carry):
            p = pl.multiple_of(s * BLK, BLK)
            values = jnp.concatenate(
                [returned[d, pl.ds(s, 1), :] for d in range(8)], axis=0
            )
            values = jnp.where(lanes + p < counts[...], values, 0.0)
            upper = (cell[:, pl.ds(p, BLK)] & (BLK - 1)) // 32
            coarse_part = jnp.concatenate(
                [jnp.where(upper == h, values, 0.0) for h in range(4)], axis=0
            )
            high = coarse_part.astype(jnp.bfloat16)
            low = (coarse_part - high.astype(jnp.float32)).astype(jnp.bfloat16)
            out = lax.dot_general(
                jnp.concatenate([high, low], axis=0), hot_spread[s],
                (((1,), (1,)), ((), ())), preferred_element_type=jnp.float32,
            )
            out = out[:32] + out[32:]
            left = jnp.take_along_axis(
                out[:, :BLK], fold_index, axis=1, mode="promise_in_bounds"
            )
            right = jnp.take_along_axis(
                out[:, BLK:], fold_index, axis=1, mode="promise_in_bounds"
            )
            out = jnp.where(fold_left, left, jnp.where(fold_right, right, 0.0))
            out = jnp.sum(out.reshape(4, 8, BLK), axis=0)
            spread[pl.ds(pl.multiple_of(s * 8, 8), 8)] = out
            return carry

        lax.fori_loop(0, slots, spread_some, 0, unroll=32)
        both = jnp.dot(
            choose[...], split_two(spread[...]), preferred_element_type=jnp.float32
        )
        added = both[:, :BLK] + both[:, BLK:]
        for z in range(zblocks):
            p = z * BLK
            field[2, 1:cx + 1, :, p:p + BLK] = (
                field[2, 1:cx + 1, :, p:p + BLK]
                + added[z * cells:(z + 1) * cells].reshape(cx, cy, BLK)
            )
        for i in range(cx):
            put_edges(last_out, 0, i, field[2, i + 1])
        start_items(early_items)
        residual_inside(2)
        for i in range(cx):
            field[3, i + 1] = partial[i]
        smoother_inside(3, 2)
        for i in range(cx):
            put_edges(last_out, 1, i, field[3, i + 1])
            put_edges(last_out, 2, i, partial[i])
        for c in range(4):
            i, j, di, dj = corner_cell(c)
            put_column(tip_out, c, 0, field[2, i + 1][j:j + 1])
            put_column(tip_out, c, zblocks, field[2, i + 1][j + dj:j + dj + 1])
            put_column(tip_out, c, 2 * zblocks, field[2, i + 1 + di][j:j + 1])
            put_column(tip_out, c, 3 * zblocks, field[3, i + 1][j:j + 1])
        start_items(last_items)
        for t in range(3):
            wait_items(edge_items(t))
        wait_items(early_items)
        wait_items(last_items)

        beyond = [layer(last_in, s, 0) for s in range(4)]
        for s in range(4):
            set_ghost(2, s, beyond[s])
        corner_resid = []
        for c in range(4):
            i, j, _, _ = corner_cell(c)
            sx, sy = (0 if i == 0 else 1), (2 if j == 0 else 3)
            value = (
                column(tip_in, c, 3 * zblocks) + beyond[sx][j:j + 1] + beyond[sy][i:i + 1]
            )
            corner_resid.append(jnp.where(exists[CORNERS[c]], value, 0.0))

        for s in range(4):
            low, high = ends[s]
            low_face, high_face = along[s]
            place = 0 if s % 2 == 0 else cy - 1
            low_side, high_side = (2, 3) if s < 2 else (0, 1)
            change = layer(last_out, s, 0) + at_ends(
                column(tip_in, low, 0), column(tip_in, high, 0)
            )
            beyond_resid = jnp.where(
                side_exists[s], layer(last_in, s, 1) + change, 0.0
            )
            set_ghost(3, s, beyond_resid)
            own_resid = layer(last_out, s, 1) + beyond[s] + at_ends(
                beyond[low_side][place:place + 1], beyond[high_side][place:place + 1]
            )
            wide = (cy, nz)
            before = jnp.where(
                first_row, jnp.broadcast_to(corner_resid[low], wide), pltpu.roll(change, 1, 0)
            )
            after = jnp.where(
                last_row, jnp.broadcast_to(corner_resid[high], wide),
                pltpu.roll(change, cy - 1, 0),
            )
            column_low = zblocks if s >= 2 else 2 * zblocks
            second = at_ends(
                column(tip_in, low, column_low), column(tip_in, high, column_low)
            )
            set_ghost(4, s, (
                layer(last_in, s, 2)
                + edges_in[s, 0] * change
                + edges_in[s, low_face] * before
                + edges_in[s, high_face] * after
                + edges_in[s, facing[s]] * own_resid
                + edges_in[s, away[s]] * second
                + edges_in[s, 5] * jnp.where(lane_ids == 0, 0.0, pltpu.roll(change, 1, 1))
                + edges_in[s, 6] * jnp.where(lane_ids == nz - 1, 0.0, pltpu.roll(change, nz - 1, 1))
            ))
        for i in range(cx):
            partial[i] = field[3, i + 1]
        for i in range(cx):
            field[3, i + 1] = residual_row(2, i)
        smoother_inside(3, 2)
        for i in range(cx):
            value = smoother_row(3, i)
            field[4, i + 1] = value
            sol_ref[i] = value
        residual_inside(4)
        for i in range(cx):
            res_ref[i] = residual_row(4, i)

        finish_items(first_items)
        finish_items(early_items)
        finish_items(last_items)
        for t in range(3):
            finish_items(edge_items(t))
        for plan in (slot_plan, back_plan, rim_plan(0), rim_plan(1), rim_plan(2)):
            for d in range(8):
                @pl.when(exists[d])
                def _():
                    eight_copy(*plan, d).wait_send()

    f32, i32, bf16 = jnp.float32, jnp.int32, jnp.bfloat16
    vm = pltpu.VMEM
    dma = pltpu.SemaphoreType.DMA
    scratch = [
        vm((ki * 8 * slots, crows), bf16), vm((slots, 256, BLK), bf16),
        pltpu.SMEM((1, 1, 8), i32), vm((8, BLK), i32),
        vm((5, cx + 2, cy, nz), f32), vm((5, 2, cx, nz), f32),
        vm((cx, cy, nz), f32), vm((cx, cy, nz), f32), vm((6, cx, cy, nz), f32),
        vm((4, 7, 8, nz), f32),
        vm((8, cap), i32), vm((kr, crows, BLK), i32), vm((kr, crows, BLK), f32),
        vm((ka, crows, BLK), i32), vm((crows, BLK), f32), vm((ka, crows, BLK), f32),
        vm((crows, BLK), f32), vm((ka, crows, BLK), f32),
        vm((ki, 8, cap), i32), vm((ki, 8, cap), f32),
        vm((ki, cx, cy, nz), i32), vm((ki, cx, cy, nz), f32),
        vm((cx, cy, nz), f32), vm((fine_rows, 2 * BLK), bf16),
        vm((fine_rows, 8 * slots), bf16),
        vm((8, slots, BLK), f32), vm((8, slots, BLK), f32),
        vm((8, slots, BLK), f32), vm((8, slots, BLK), f32),
        vm((3, crows, BLK), f32), vm((3, 8, rim_rows, BLK), f32),
        vm((8 * slots, BLK), f32), vm((cx, cy, nz), f32),
        vm((4, (3 * 8 + 2) * zblocks, BLK), f32), vm((4, (3 * 8 + 2) * zblocks, BLK), f32),
        vm((4, zblocks, BLK), f32), vm((4, zblocks, BLK), f32),
        vm((4, 3 * 8 * zblocks, BLK), f32), vm((4, 3 * 8 * zblocks, BLK), f32),
        vm((4, 4 * zblocks, BLK), f32), vm((4, 4 * zblocks, BLK), f32),
        vm((4, 7, 8, nz), f32),
        dma((25,)), dma((4,)), dma((4,)), dma((4,)), dma((4,)), dma((2, 4)), dma((2, 4)),
        dma((4,)), dma((4,)), dma((3, 4)), dma((3, 4)),
        dma((8,)), dma((8,)), dma((8,)), dma((8,)),
        dma((3, 8)), dma((3, 8)),
    ]
    whole = pl.BlockSpec(memory_space=pltpu.VMEM)
    in_hbm = pl.BlockSpec(memory_space=pltpu.HBM)
    return pl.pallas_call(
        kernel,
        out_shape=(
            jax.ShapeDtypeStruct((cx, cy, nz), f32),
            jax.ShapeDtypeStruct((cx, cy, nz), f32),
        ),
        in_specs=[in_hbm] * 17,
        out_specs=(whole, whole),
        scratch_shapes=scratch,
        compiler_params=pltpu.CompilerParams(
            collective_id=0, has_side_effects=True, vmem_limit_bytes=40 * 1024 * 1024
        ),
        name="vcycle",
    )


def write_out(first, second):
    def kernel(first_ref, second_ref, first_out, second_out, sem):
        copies = [
            pltpu.make_async_copy(first_ref, first_out, sem.at[0]),
            pltpu.make_async_copy(second_ref, second_out, sem.at[1]),
        ]
        for copy in copies:
            copy.start()
        for copy in copies:
            copy.wait()

    return pl.pallas_call(
        kernel,
        out_shape=(
            jax.ShapeDtypeStruct(first.shape, first.dtype),
            jax.ShapeDtypeStruct(second.shape, second.dtype),
        ),
        in_specs=[pl.BlockSpec(memory_space=pltpu.VMEM)] * 2,
        out_specs=(pl.BlockSpec(memory_space=pltpu.HBM),) * 2,
        scratch_shapes=[pltpu.SemaphoreType.DMA((2,))],
        compiler_params=pltpu.CompilerParams(vmem_limit_bytes=4 * 1024 * 1024),
        name="write_out",
    )(first, second)


def body(
    rhs, diag, smoother_center, smoother_faces, send_count, send_cell, restrict_col,
    restrict_vals, coarse_col, coarse_diag, coarse_vals, csmooth_diag, csmooth_vals,
    remote_row, remote_vals, interp_row, interp_vals,
):
    def rows(array):
        return array.reshape(array.shape[0], -1, BLK)

    cap = send_cell.shape[-1]
    ki = remote_row.shape[0]
    def in_hbm(array):
        return pltpu.with_memory_space_constraint(array, pltpu.HBM)

    operands = (
        rhs, diag, smoother_center, smoother_faces,
        send_count,
        send_cell.reshape(8, cap), rows(restrict_col), rows(restrict_vals),
        rows(coarse_col), coarse_diag.reshape(-1, BLK), rows(coarse_vals),
        csmooth_diag.reshape(-1, BLK), rows(csmooth_vals),
        remote_row.reshape(ki, 8, cap), remote_vals.reshape(ki, 8, cap),
        interp_row, interp_vals,
    )
    shapes = {
        "rhs": rhs.shape, "send_cell": (8, cap), "restrict_col": operands[6].shape,
        "coarse_col": operands[8].shape, "interp_row": interp_row.shape,
    }
    sizes = (lax.axis_size("gx"), lax.axis_size("gy"))
    operands = [in_hbm(x) for x in operands]
    return write_out(*make_kernel(sizes, shapes)(*operands))


def solution(mesh):
    fine = P("gx", "gy", None)
    listed = P(None, "gx", "gy", None)
    placed = (
        fine, fine, fine, listed, fine, P("gx", "gy", None, None), listed, listed,
        listed, fine, listed, fine, listed,
        P(None, "gx", "gy", None, None), P(None, "gx", "gy", None, None),
        listed, listed,
    )
    return jax.shard_map(
        body, mesh=mesh, in_specs=placed, out_specs=(fine, fine), check_vma=False
    )
```

```python
import jax
import jax.numpy as jnp
from jax import lax
from jax.experimental import pallas as pl
from jax.experimental.pallas import tpu as pltpu
from jax.sharding import PartitionSpec as P

BLK = 128
OFFSETS = ((-1, -1), (-1, 0), (-1, 1), (0, -1), (0, 1), (1, -1), (1, 0), (1, 1))
SIDES = ((-1, 0), (1, 0), (0, -1), (0, 1))
CORNERS = (0, 2, 5, 7)
MESH_ID = pl.DeviceIdType.MESH


def split_two(table):
    high = table.astype(jnp.bfloat16)
    low = (table - high.astype(jnp.float32)).astype(jnp.bfloat16)
    return jnp.concatenate([high, low], axis=1)


def one_hot(base, width):
    ids = lax.broadcasted_iota(jnp.int32, (base.shape[0], width), 1)
    return jnp.where(ids == base, 1.0, 0.0).astype(jnp.bfloat16)


def pick(index, base, table_two):
    return pick_hot(index, one_hot(base, table_two.shape[0]), table_two)


def pick_hot(index, hot, table_two):
    both = jnp.dot(hot, table_two, preferred_element_type=jnp.float32)
    rows = both[:, :BLK] + both[:, BLK:]
    return jnp.take_along_axis(rows, index & (BLK - 1), axis=1, mode="promise_in_bounds")


def make_kernel(sizes, shapes):
    na, nb = sizes
    cx, cy, nz = shapes["rhs"]
    zblocks = nz // BLK
    cells = cx * cy
    fine_rows = cells * zblocks
    cap = shapes["send_cell"][1]
    slots = cap // BLK
    kr, crows, _ = shapes["restrict_col"]
    ka = shapes["coarse_col"][0]
    ki = shapes["interp_row"][0]
    rim_rows = 8

    def fine_place(block):
        return (block % zblocks) * cells + block // zblocks

    def kernel(
        rhs_h, diag_h, center_h, faces_h, count_h, cell_h, rcol_h, rval_h, ccol_h,
        cdiag_h, cval_h, mdiag_h, mval_h, rrow_h, rrval_h, irow_h, ival_h,
        sol_ref, res_ref,
        hot_back, hot_spread, turned, count, counts, field, yrecv, diag, center, faces, edges, cell, rcol, rval, ccol, cdiag, cval,
        mdiag, mval, rrow, rrval, irow, ival, resid, fine_two, choose, sent, received,
        back, returned, coarse, rim, spread, partial,
        first_out, first_in, pre_out, pre_in, last_out, last_in, tip_out, tip_in, edges_in,
        ends_out, ends_in, in_sem, first_send, first_recv, pre_send, pre_recv, last_send, last_recv,
        tip_send, tip_recv, edges_send, edges_recv,
        slot_send, slot_recv, back_send, back_recv, rim_send, rim_recv,
    ):
        a = lax.axis_index("gx")
        b = lax.axis_index("gy")

        loads = [
            (rhs_h, field.at[0, pl.ds(1, cx)]), (center_h, center), (faces_h, faces),
            (center_h.at[0], edges.at[0, 0]), (center_h.at[cx - 1], edges.at[1, 0]),
            (center_h.at[:, 0, :], edges.at[2, 0]), (center_h.at[:, cy - 1, :], edges.at[3, 0]),
            (faces_h.at[pl.ds(2, 4), 0], edges.at[0, pl.ds(1, 4)]),
            (faces_h.at[pl.ds(2, 4), cx - 1], edges.at[1, pl.ds(1, 4)]),
            (faces_h.at[pl.ds(0, 2), :, 0, :], edges.at[2, pl.ds(1, 2)]),
            (faces_h.at[pl.ds(4, 2), :, 0, :], edges.at[2, pl.ds(3, 2)]),
            (faces_h.at[pl.ds(0, 2), :, cy - 1, :], edges.at[3, pl.ds(1, 2)]),
            (faces_h.at[pl.ds(4, 2), :, cy - 1, :], edges.at[3, pl.ds(3, 2)]),
            (diag_h, diag), (cell_h, cell), (count_h, count), (rcol_h, rcol), (rval_h, rval),
            (ccol_h, ccol), (mdiag_h, mdiag), (mval_h, mval), (cdiag_h, cdiag),
            (cval_h, cval), (rrow_h, rrow), (rrval_h, rrval), (irow_h, irow),
            (ival_h, ival),
        ]
        loads = [
            pltpu.make_async_copy(source, target, in_sem.at[n])
            for n, (source, target) in enumerate(loads)
        ]

        def there(step):
            dx, dy = step
            checks = []
            if dx < 0:
                checks.append(a > 0)
            if dx > 0:
                checks.append(a < na - 1)
            if dy < 0:
                checks.append(b > 0)
            if dy > 0:
                checks.append(b < nb - 1)
            out = checks[0]
            for check in checks[1:]:
                out = jnp.logical_and(out, check)
            return out

        exists = [there(step) for step in OFFSETS]
        side_exists = [there(step) for step in SIDES]

        barrier = pltpu.get_barrier_semaphore()
        total = jnp.int32(0)
        for d, (dx, dy) in enumerate(OFFSETS):
            @pl.when(exists[d])
            def _():
                pl.semaphore_signal(
                    barrier, inc=1, device_id=(a + dx, b + dy), device_id_type=MESH_ID
                )
            total = total + exists[d].astype(jnp.int32)

        for load in loads[:3]:
            load.start()

        def item(cond, step, src, there_ref, here_ref, send, there_sem, here_sem):
            target = (a + step[0], b + step[1])

            def copy():
                return pltpu.make_async_remote_copy(
                    src_ref=src, dst_ref=there_ref, send_sem=send, recv_sem=there_sem,
                    device_id=target, device_id_type=MESH_ID,
                )

            def arrival():
                return pltpu.make_async_remote_copy(
                    src_ref=here_ref, dst_ref=here_ref, send_sem=send, recv_sem=here_sem,
                    device_id=target, device_id_type=MESH_ID,
                )

            return cond, copy, arrival

        def side_items(out, into, send, recv):
            return [
                item(
                    side_exists[s], SIDES[s], out(s), into(s ^ 1), into(s),
                    send(s), recv(s ^ 1), recv(s),
                )
                for s in (2, 3, 0, 1)
            ]

        def corner_items(out, into, send, recv):
            return [
                item(
                    exists[CORNERS[c]], OFFSETS[CORNERS[c]], out.at[c], into.at[3 - c],
                    into.at[c], send.at[c], recv.at[3 - c], recv.at[c],
                )
                for c in range(4)
            ]

        first_items = corner_items(pre_out, pre_in, pre_send, pre_recv) + side_items(
            lambda s: first_out.at[s], lambda s: first_in.at[s],
            lambda s: first_send.at[s], lambda s: first_recv.at[s],
        )
        part = 8 * zblocks
        early_items = side_items(
            lambda s: last_out.at[s, pl.ds(0, part)], lambda s: last_in.at[s, pl.ds(0, part)],
            lambda s: last_send.at[0, s], lambda s: last_recv.at[0, s],
        )
        last_items = corner_items(tip_out, tip_in, tip_send, tip_recv) + side_items(
            lambda s: last_out.at[s, pl.ds(part, 2 * part)],
            lambda s: last_in.at[s, pl.ds(part, 2 * part)],
            lambda s: last_send.at[1, s], lambda s: last_recv.at[1, s],
        )

        def edge_items(t):
            if t == 3:
                return side_items(
                    lambda s: ends_out.at[s], lambda s: ends_in.at[s],
                    lambda s: edges_send.at[t, s], lambda s: edges_recv.at[t, s],
                )
            low, size = ((0, 2), (2, 2), (4, 1))[t]
            items = side_items(
                lambda s: edges.at[s, pl.ds(low, size)],
                lambda s: edges_in.at[s, pl.ds(low, size)],
                lambda s: edges_send.at[t, s], lambda s: edges_recv.at[t, s],
            )[0:2]
            if t == 0:
                items = items + side_items(
                    lambda s: edges.at[s], lambda s: edges_in.at[s],
                    lambda s: edges_send.at[t, s], lambda s: edges_recv.at[t, s],
                )[2:4]
            return items

        def start_items(items):
            for cond, copy, _ in items:
                @pl.when(cond)
                def _():
                    copy().start()

        def wait_items(items):
            for cond, _, arrival in items:
                @pl.when(cond)
                def _():
                    arrival().wait_recv()

        def finish_items(items):
            for cond, copy, _ in items:
                @pl.when(cond)
                def _():
                    copy().wait_send()

        def eight_copy(src, dst, send_sem, recv_sem, d):
            dx, dy = OFFSETS[d]
            return pltpu.make_async_remote_copy(
                src_ref=src(d), dst_ref=dst(7 - d), send_sem=send_sem(d),
                recv_sem=recv_sem(7 - d),
                device_id=(a + dx, b + dy), device_id_type=MESH_ID,
            )

        def eight_arrival(dst, send_sem, recv_sem, d):
            dx, dy = OFFSETS[d]
            return pltpu.make_async_remote_copy(
                src_ref=dst(d), dst_ref=dst(d), send_sem=send_sem(d), recv_sem=recv_sem(d),
                device_id=(a + dx, b + dy), device_id_type=MESH_ID,
            )

        slot_plan = (
            lambda d: sent.at[d], lambda d: received.at[d],
            lambda d: slot_send.at[d], lambda d: slot_recv.at[d],
        )
        back_plan = (
            lambda d: back.at[d], lambda d: returned.at[d],
            lambda d: back_send.at[d], lambda d: back_recv.at[d],
        )

        def rim_plan(t):
            return (
                lambda d: coarse.at[t, pl.ds(0, rim_rows)], lambda d: rim.at[t, d],
                lambda d: rim_send.at[t, d], lambda d: rim_recv.at[t, d],
            )

        def start_eight(plan):
            for d in (0, 2, 5, 7, 3, 4, 1, 6):
                @pl.when(exists[d])
                def _():
                    eight_copy(*plan, d).start()

        def wait_eight(plan):
            for d in range(8):
                @pl.when(exists[d])
                def _():
                    eight_arrival(*plan[1:], d).wait_recv()

        row_ids = lax.broadcasted_iota(jnp.int32, (cy, nz), 0)
        lane_ids = lax.broadcasted_iota(jnp.int32, (cy, nz), 1)

        zeros = jnp.zeros((cy, nz), jnp.float32)

        def beside(t, i):
            centre = field[t, i + 1]
            return centre, [
                field[t, i] if i > 0 else zeros,
                field[t, i + 2] if i < cx - 1 else zeros,
                jnp.where(row_ids == 0, 0.0, pltpu.roll(centre, 1, 0)),
                jnp.where(row_ids == cy - 1, 0.0, pltpu.roll(centre, cy - 1, 0)),
                jnp.where(lane_ids == 0, 0.0, pltpu.roll(centre, 1, 1)),
                jnp.where(lane_ids == nz - 1, 0.0, pltpu.roll(centre, nz - 1, 1)),
            ]

        def sides(t, i):
            out = [
                jnp.where(row_ids == 0, jnp.broadcast_to(yrecv[t, 0, i:i + 1, :], (cy, nz)), 0.0),
                jnp.where(row_ids == cy - 1, jnp.broadcast_to(yrecv[t, 1, i:i + 1, :], (cy, nz)), 0.0),
            ]
            return [
                field[t, 0] if i == 0 else None,
                field[t, cx + 1] if i == cx - 1 else None,
            ] + out

        def residual_inside(t):
            for i in range(cx):
                centre, near = beside(t, i)
                sums = near[0]
                for one in near[1:]:
                    sums = sums + one
                partial[i] = field[0, i + 1] - ((6.0 + diag[i]) * centre - sums)

        def residual_row(t, i):
            out = partial[i]
            for one in sides(t, i):
                if one is not None:
                    out = out + one
            return out

        def smoother_inside(t, base):
            for i in range(cx):
                centre, near = beside(t, i)
                out = center[i] * centre
                for q in range(6):
                    out = out + faces[q, i] * near[q]
                partial[i] = out if base is None else field[base, i + 1] + out

        def smoother_row(t, i):
            out = partial[i]
            for q, one in enumerate(sides(t, i)):
                if one is not None:
                    out = out + faces[q, i] * one
            return out

        def put_edges(out, n, i, value):
            base = n * zblocks * 8
            for z in range(zblocks):
                part = value[:, z * BLK:(z + 1) * BLK]
                row = base + z * 8
                if i == 0:
                    out[0, row:row + 8, :] = part
                if i == cx - 1:
                    out[1, row:row + 8, :] = part
                out[2, row + i:row + i + 1, :] = part[0:1]
                out[3, row + i:row + i + 1, :] = part[cy - 1:cy]

        def layer(ref, s, n):
            base = n * zblocks * 8
            return jnp.concatenate(
                [ref[s, base + 8 * z:base + 8 * z + 8, :] for z in range(zblocks)], axis=1
            )

        def column(ref, c, low, step=1):
            return jnp.concatenate(
                [ref[c, low + z * step:low + z * step + 1, :] for z in range(zblocks)], axis=1
            )

        def put_column(ref, c, low, value):
            for z in range(zblocks):
                ref[c, low + z:low + z + 1, :] = value[:, z * BLK:(z + 1) * BLK]

        def corner_cell(c):
            dx, dy = OFFSETS[CORNERS[c]]
            return (0 if dx < 0 else cx - 1), (0 if dy < 0 else cy - 1), -dx, -dy

        ends = [(0, 1), (2, 3), (0, 2), (1, 3)]
        first_row, last_row = row_ids == 0, row_ids == cy - 1

        def at_ends(low, high):
            wide = (cy, nz)
            return jnp.where(
                first_row, jnp.broadcast_to(low, wide),
                jnp.where(last_row, jnp.broadcast_to(high, wide), 0.0),
            )

        for load in loads[0:3]:
            load.wait()
        for load in loads[3:]:
            load.start()
        smoother_inside(0, None)
        for i in range(cx):
            put_edges(first_out, 0, i, field[0, i + 1])
            put_edges(first_out, 1, i, partial[i])
        for c in range(4):
            i, j, _, _ = corner_cell(c)
            put_column(pre_out, c, 0, field[0, i + 1][j:j + 1])
        end_row = 3 * zblocks * 8
        face_rows = 2 * zblocks * 8
        for z in range(zblocks):
            p = z * BLK
            row = face_rows + z * 8
            first_out[0, row:row + 8, :] = faces[0, 0, :, p:p + BLK]
            first_out[1, row:row + 8, :] = faces[1, cx - 1, :, p:p + BLK]
            for i in range(cx):
                first_out[2, row + i:row + i + 1, :] = faces[2, i, 0:1, p:p + BLK]
                first_out[3, row + i:row + i + 1, :] = faces[3, i, cy - 1:cy, p:p + BLK]
            for s in range(4):
                place = (0 if s % 2 == 0 else (cx if s < 2 else cy) - 1)
                if s < 2:
                    at_low = faces[2, place, 0:1, p:p + BLK]
                    at_high = faces[3, place, cy - 1:cy, p:p + BLK]
                else:
                    at_low = faces[0, 0, place:place + 1, p:p + BLK]
                    at_high = faces[1, cx - 1, place:place + 1, p:p + BLK]
                first_out[s, end_row + z:end_row + z + 1, :] = at_low
                row_high = end_row + zblocks + z
                first_out[s, row_high:row_high + 1, :] = at_high
        pl.semaphore_wait(barrier, total)
        start_items(first_items)
        for s in range(4):
            @pl.when(jnp.logical_not(side_exists[s]))
            def _():
                first_in[s] = jnp.zeros(first_in.shape[1:], jnp.float32)
                last_in[s] = jnp.zeros(last_in.shape[1:], jnp.float32)
                edges_in[s] = jnp.zeros(edges_in.shape[1:], jnp.float32)
                ends_in[s] = jnp.zeros(ends_in.shape[1:], jnp.float32)
        for c in range(4):
            @pl.when(jnp.logical_not(exists[CORNERS[c]]))
            def _():
                pre_in[c] = jnp.zeros(pre_in.shape[1:], jnp.float32)
                tip_in[c] = jnp.zeros(tip_in.shape[1:], jnp.float32)
        for d in range(8):
            @pl.when(jnp.logical_not(exists[d]))
            def _():
                received[d] = jnp.zeros((slots, BLK), jnp.float32)
                returned[d] = jnp.zeros((slots, BLK), jnp.float32)
                for t in range(3):
                    rim[t, d] = jnp.zeros((rim_rows, BLK), jnp.float32)

        edge_loads, loads = loads[3:13], loads[12:]
        for load in loads[1:4]:
            load.wait()
        slot_rows = lax.broadcasted_iota(jnp.int32, (8, BLK), 0)
        value = jnp.zeros((8, BLK), jnp.int32)
        for d in range(8):
            value = jnp.where(slot_rows == d, count[0, 0, d], value)
        counts[...] = value

        cell_index = jnp.concatenate(
            [cell[:, s * BLK:(s + 1) * BLK] for s in range(slots)], axis=0
        )
        cell_base = fine_place(cell_index[:, 0:1] // BLK)
        across = jnp.transpose(
            jnp.broadcast_to(cell_base, (8 * slots, BLK)).astype(jnp.float32)
        )[0:1].astype(jnp.int32)
        fine_ids = lax.broadcasted_iota(jnp.int32, (fine_rows, 8 * slots), 0)
        choose[...] = jnp.where(fine_ids == across, 1.0, 0.0).astype(jnp.bfloat16)
        hot_slot = one_hot(cell_base, fine_rows)

        for load in loads[4:] + edge_loads:
            load.wait()
        group = 8 if slots % 8 == 0 else 1
        batch = group * ki * 8

        def back_index(c):
            parts = [(c * group + g) * BLK for g in range(group)]
            return jnp.concatenate(
                [rrow[:, :, p:p + BLK].reshape(ki * 8, BLK) for p in parts], axis=0
            )

        for c in range(slots // group):
            hot_back[c * batch:(c + 1) * batch] = one_hot(back_index(c)[:, 0:1] // BLK, crows)

        for s in range(4):
            place = (0 if s % 2 == 0 else (cx if s < 2 else cy) - 1)
            for z in range(zblocks):
                p = z * BLK
                if s < 2:
                    at_low = faces[s ^ 1, place, 0:1, p:p + BLK]
                    at_high = faces[s ^ 1, place, cy - 1:cy, p:p + BLK]
                else:
                    at_low = faces[s ^ 1, 0, place:place + 1, p:p + BLK]
                    at_high = faces[s ^ 1, cx - 1, place:place + 1, p:p + BLK]
                ends_out[s, z:z + 1, :] = at_low
                ends_out[s, zblocks + z:zblocks + z + 1, :] = at_high
        low_ids = lax.broadcasted_iota(jnp.int32, (32, BLK), 0)

        def scatter_some(s, carry):
            lower = cell[:, pl.ds(pl.multiple_of(s * BLK, BLK), BLK)] & 31
            hot_spread[s] = jnp.concatenate(
                [
                    jnp.where(jnp.broadcast_to(lower[d:d + 1], (32, BLK)) == low_ids, 1.0, 0.0)
                    for d in range(8)
                ],
                axis=0,
            ).astype(jnp.bfloat16)
            return carry

        lax.fori_loop(0, slots, scatter_some, 0, unroll=4)
        wait_items(first_items)

        def set_ghost(t, s, value):
            if s < 2:
                field[t, 0 if s == 0 else cx + 1] = value
            else:
                yrecv[t, s - 2] = value

        for s in range(4):
            set_ghost(0, s, layer(first_in, s, 0))
            low, high = ends[s]
            set_ghost(1, s, (
                layer(first_in, s, 1) + layer(first_in, s, 2) * layer(first_out, s, 0)
                + at_ends(
                    column(first_in, s, end_row) * column(pre_in, low, 0),
                    column(first_in, s, end_row + zblocks) * column(pre_in, high, 0),
                )
            ))
        for i in range(cx):
            field[1, i + 1] = smoother_row(0, i)
        residual_inside(1)
        for i in range(cx):
            resid[i] = residual_row(1, i)
        table = jnp.concatenate(
            [resid[:, :, z * BLK:(z + 1) * BLK].reshape(cells, BLK) for z in range(zblocks)],
            axis=0,
        )
        fine_two[...] = split_two(table)

        picked = pick_hot(cell_index, hot_slot, fine_two[...])
        lanes = lax.broadcasted_iota(jnp.int32, (8, BLK), 1)
        slot_ids = lax.broadcasted_iota(jnp.int32, (slots, 8, BLK), 0) * BLK + lanes[None]
        values = jnp.where(
            slot_ids < counts[...][None], picked.reshape(slots, 8, BLK), 0.0
        )
        sent[...] = jnp.swapaxes(values, 0, 1)
        start_eight(slot_plan)

        step = 9 if kr % 9 == 0 else 1

        def restrict_some(c, acc):
            index = rcol[pl.ds(c * step, step)].reshape(step * crows, BLK)
            block = index[:, 0:1] // BLK
            base = jnp.where(block < fine_rows, fine_place(block), -1)
            got = pick(index, base, fine_two[...]).reshape(step, crows, BLK)
            return acc + jnp.sum(got * rval[pl.ds(c * step, step)], axis=0)

        rc = lax.fori_loop(
            0, kr // step, restrict_some, jnp.zeros((crows, BLK), jnp.float32)
        )
        far_index = rcol[:, 0:rim_rows, :].reshape(kr * rim_rows, BLK)
        hot_far = one_hot(far_index[:, 0:1] // BLK - fine_rows, 8 * slots)
        own_index = ccol[...].reshape(ka * crows, BLK)
        hot_own = one_hot(own_index[:, 0:1] // BLK, crows)
        rim_index = ccol[:, 0:rim_rows, :].reshape(ka * rim_rows, BLK)
        hot_rim = one_hot(rim_index[:, 0:1] // BLK - crows, 8 * rim_rows)
        wait_eight(slot_plan)
        received_two = split_two(received[...].reshape(8 * slots, BLK))
        got = pick_hot(far_index, hot_far, received_two)
        more = jnp.sum(
            got.reshape(kr, rim_rows, BLK) * rval[:, 0:rim_rows, :], axis=0
        )
        rc = jnp.concatenate([rc[:rim_rows] + more, rc[rim_rows:]], axis=0)

        def coarse_apply(t, vector, diagonal, values):
            coarse[t] = vector
            start_eight(rim_plan(t))
            start_items(edge_items(t))
            if t == 2:
                start_items(edge_items(3))
            got = pick_hot(own_index, hot_own, split_two(vector))
            own = diagonal[...] * vector + jnp.sum(
                got.reshape(ka, crows, BLK) * values[...], axis=0
            )
            wait_eight(rim_plan(t))
            got = pick_hot(
                rim_index, hot_rim, split_two(rim[t].reshape(8 * rim_rows, BLK))
            )
            more = jnp.sum(
                got.reshape(ka, rim_rows, BLK) * values[:, 0:rim_rows, :], axis=0
            )
            return jnp.concatenate([own[:rim_rows] + more, own[rim_rows:]], axis=0)

        xc1 = coarse_apply(0, rc, mdiag, mval)
        rc2 = rc - coarse_apply(1, xc1, cdiag, cval)
        xc2 = xc1 + coarse_apply(2, rc2, mdiag, mval)
        coarse_two = split_two(xc2)

        for c in range(slots // group):
            parts = [(c * group + g) * BLK for g in range(group)]
            got = pick_hot(
                back_index(c), hot_back[c * batch:(c + 1) * batch], coarse_two
            )
            values = []
            for g, p in enumerate(parts):
                mine = got[g * ki * 8:(g + 1) * ki * 8].reshape(ki, 8, BLK)
                values.append(jnp.sum(mine * rrval[:, :, p:p + BLK], axis=0))
            back[:, c * group:(c + 1) * group, :] = jnp.swapaxes(jnp.stack(values), 0, 1)
        start_eight(back_plan)

        for z in range(zblocks):
            p = z * BLK
            index = irow[:, :, :, p:p + BLK].reshape(ki * cells, BLK)
            got = pick(index, index[:, 0:1] // BLK, coarse_two)
            got = got.reshape(ki, cx, cy, BLK) * ival[:, :, :, p:p + BLK]
            field[2, 1:cx + 1, :, p:p + BLK] = (
                field[1, 1:cx + 1, :, p:p + BLK] + jnp.sum(got, axis=0)
            )
        wait_eight(back_plan)

        in_place = lanes // 32 == slot_rows % 4

        def spread_some(s, carry):
            p = pl.multiple_of(s * BLK, BLK)
            values = jnp.where(lanes + p < counts[...], turned[s], 0.0)
            high = values.astype(jnp.bfloat16).astype(jnp.float32)
            low = values - high
            turn = ((cell[:, pl.ds(p, BLK)] & (BLK - 1)) // 32 - slot_rows) & 3
            left_side = jnp.concatenate(
                [jnp.where(turn == h, part, 0.0) for part in (high, low) for h in range(4)],
                axis=0,
            ).astype(jnp.bfloat16)
            both = lax.dot_general(
                left_side, hot_spread[s], (((1,), (1,)), ((), ())),
                preferred_element_type=jnp.float32,
            )
            both = both[:32] + both[32:]
            out = jnp.zeros((8, BLK), jnp.float32)
            for h in range(4):
                near = both[8 * h:8 * h + 8]
                near = jnp.where(slot_rows < 4, near[:, :BLK], near[:, BLK:])
                near = jnp.where(in_place, near, 0.0)
                out = out + (pltpu.roll(near, 32 * h, 1) if h else near)
            spread[pl.ds(pl.multiple_of(s * 8, 8), 8)] = out
            return carry

        turned[...] = jnp.swapaxes(returned[...], 0, 1)
        lax.fori_loop(0, slots, spread_some, 0, unroll=32)
        both = jnp.dot(
            choose[...], split_two(spread[...]), preferred_element_type=jnp.float32
        )
        added = both[:, :BLK] + both[:, BLK:]
        for z in range(zblocks):
            p = z * BLK
            field[2, 1:cx + 1, :, p:p + BLK] = (
                field[2, 1:cx + 1, :, p:p + BLK]
                + added[z * cells:(z + 1) * cells].reshape(cx, cy, BLK)
            )
        for i in range(cx):
            put_edges(last_out, 0, i, field[2, i + 1])
        start_items(early_items)
        residual_inside(2)
        for i in range(cx):
            field[3, i + 1] = partial[i]
        smoother_inside(3, 2)
        for i in range(cx):
            put_edges(last_out, 1, i, field[3, i + 1])
            put_edges(last_out, 2, i, partial[i])
        for c in range(4):
            i, j, di, dj = corner_cell(c)
            put_column(tip_out, c, 0, field[2, i + 1][j:j + 1])
            put_column(tip_out, c, zblocks, field[2, i + 1][j + dj:j + dj + 1])
            put_column(tip_out, c, 2 * zblocks, field[2, i + 1 + di][j:j + 1])
            put_column(tip_out, c, 3 * zblocks, field[3, i + 1][j:j + 1])
        start_items(last_items)
        for t in range(4):
            wait_items(edge_items(t))
        wait_items(early_items)
        wait_items(last_items)

        beyond = [layer(last_in, s, 0) for s in range(4)]
        for s in range(4):
            set_ghost(2, s, beyond[s])
        corner_resid = []
        for c in range(4):
            i, j, _, _ = corner_cell(c)
            sx, sy = (0 if i == 0 else 1), (2 if j == 0 else 3)
            value = (
                column(tip_in, c, 3 * zblocks) + beyond[sx][j:j + 1] + beyond[sy][i:i + 1]
            )
            corner_resid.append(jnp.where(exists[CORNERS[c]], value, 0.0))

        for s in range(4):
            low, high = ends[s]
            place = 0 if s % 2 == 0 else cy - 1
            low_side, high_side = (2, 3) if s < 2 else (0, 1)
            change = layer(last_out, s, 0) + at_ends(
                column(tip_in, low, 0), column(tip_in, high, 0)
            )
            beyond_resid = jnp.where(
                side_exists[s], layer(last_in, s, 1) + change, 0.0
            )
            set_ghost(3, s, beyond_resid)
            own_resid = layer(last_out, s, 1) + beyond[s] + at_ends(
                beyond[low_side][place:place + 1], beyond[high_side][place:place + 1]
            )
            wide = (cy, nz)
            before = jnp.where(
                first_row, jnp.broadcast_to(corner_resid[low], wide), pltpu.roll(change, 1, 0)
            )
            after = jnp.where(
                last_row, jnp.broadcast_to(corner_resid[high], wide),
                pltpu.roll(change, cy - 1, 0),
            )
            column_low = zblocks if s >= 2 else 2 * zblocks
            second = at_ends(
                column(ends_in, s, 0) * column(tip_in, low, column_low),
                column(ends_in, s, zblocks) * column(tip_in, high, column_low),
            )
            set_ghost(4, s, (
                layer(last_in, s, 2)
                + edges_in[s, 0] * change
                + edges_in[s, 1] * before
                + edges_in[s, 2] * after
                + layer(first_in, s, 2) * own_resid
                + second
                + edges_in[s, 3] * jnp.where(lane_ids == 0, 0.0, pltpu.roll(change, 1, 1))
                + edges_in[s, 4] * jnp.where(lane_ids == nz - 1, 0.0, pltpu.roll(change, nz - 1, 1))
            ))
        for i in range(cx):
            partial[i] = field[3, i + 1]
        for i in range(cx):
            field[3, i + 1] = residual_row(2, i)
        smoother_inside(3, 2)
        for i in range(cx):
            value = smoother_row(3, i)
            field[4, i + 1] = value
            sol_ref[i] = value
        residual_inside(4)
        for i in range(cx):
            res_ref[i] = residual_row(4, i)

        finish_items(first_items)
        finish_items(early_items)
        finish_items(last_items)
        for t in range(4):
            finish_items(edge_items(t))
        for plan in (slot_plan, back_plan, rim_plan(0), rim_plan(1), rim_plan(2)):
            for d in range(8):
                @pl.when(exists[d])
                def _():
                    eight_copy(*plan, d).wait_send()

    f32, i32, bf16 = jnp.float32, jnp.int32, jnp.bfloat16
    vm = pltpu.VMEM
    dma = pltpu.SemaphoreType.DMA
    scratch = [
        vm((ki * 8 * slots, crows), bf16), vm((slots, 256, BLK), bf16), vm((slots, 8, BLK), f32),
        pltpu.SMEM((1, 1, 8), i32), vm((8, BLK), i32),
        vm((5, cx + 2, cy, nz), f32), vm((5, 2, cx, nz), f32),
        vm((cx, cy, nz), f32), vm((cx, cy, nz), f32), vm((6, cx, cy, nz), f32),
        vm((4, 5, 8, nz), f32),
        vm((8, cap), i32), vm((kr, crows, BLK), i32), vm((kr, crows, BLK), f32),
        vm((ka, crows, BLK), i32), vm((crows, BLK), f32), vm((ka, crows, BLK), f32),
        vm((crows, BLK), f32), vm((ka, crows, BLK), f32),
        vm((ki, 8, cap), i32), vm((ki, 8, cap), f32),
        vm((ki, cx, cy, nz), i32), vm((ki, cx, cy, nz), f32),
        vm((cx, cy, nz), f32), vm((fine_rows, 2 * BLK), bf16),
        vm((fine_rows, 8 * slots), bf16),
        vm((8, slots, BLK), f32), vm((8, slots, BLK), f32),
        vm((8, slots, BLK), f32), vm((8, slots, BLK), f32),
        vm((3, crows, BLK), f32), vm((3, 8, rim_rows, BLK), f32),
        vm((8 * slots, BLK), f32), vm((cx, cy, nz), f32),
        vm((4, (3 * 8 + 2) * zblocks, BLK), f32), vm((4, (3 * 8 + 2) * zblocks, BLK), f32),
        vm((4, zblocks, BLK), f32), vm((4, zblocks, BLK), f32),
        vm((4, 3 * 8 * zblocks, BLK), f32), vm((4, 3 * 8 * zblocks, BLK), f32),
        vm((4, 4 * zblocks, BLK), f32), vm((4, 4 * zblocks, BLK), f32),
        vm((4, 5, 8, nz), f32),
        vm((4, 2 * zblocks, BLK), f32), vm((4, 2 * zblocks, BLK), f32),
        dma((27,)), dma((4,)), dma((4,)), dma((4,)), dma((4,)), dma((2, 4)), dma((2, 4)),
        dma((4,)), dma((4,)), dma((4, 4)), dma((4, 4)),
        dma((8,)), dma((8,)), dma((8,)), dma((8,)),
        dma((3, 8)), dma((3, 8)),
    ]
    whole = pl.BlockSpec(memory_space=pltpu.VMEM)
    in_hbm = pl.BlockSpec(memory_space=pltpu.HBM)
    return pl.pallas_call(
        kernel,
        out_shape=(
            jax.ShapeDtypeStruct((cx, cy, nz), f32),
            jax.ShapeDtypeStruct((cx, cy, nz), f32),
        ),
        in_specs=[in_hbm] * 17,
        out_specs=(whole, whole),
        scratch_shapes=scratch,
        compiler_params=pltpu.CompilerParams(
            collective_id=0, has_side_effects=True, vmem_limit_bytes=40 * 1024 * 1024
        ),
        name="vcycle",
    )


def write_out(first, second):
    def kernel(first_ref, second_ref, first_out, second_out, sem):
        copies = [
            pltpu.make_async_copy(first_ref, first_out, sem.at[0]),
            pltpu.make_async_copy(second_ref, second_out, sem.at[1]),
        ]
        for copy in copies:
            copy.start()
        for copy in copies:
            copy.wait()

    return pl.pallas_call(
        kernel,
        out_shape=(
            jax.ShapeDtypeStruct(first.shape, first.dtype),
            jax.ShapeDtypeStruct(second.shape, second.dtype),
        ),
        in_specs=[pl.BlockSpec(memory_space=pltpu.VMEM)] * 2,
        out_specs=(pl.BlockSpec(memory_space=pltpu.HBM),) * 2,
        scratch_shapes=[pltpu.SemaphoreType.DMA((2,))],
        compiler_params=pltpu.CompilerParams(vmem_limit_bytes=4 * 1024 * 1024),
        name="write_out",
    )(first, second)


def body(
    rhs, diag, smoother_center, smoother_faces, send_count, send_cell, restrict_col,
    restrict_vals, coarse_col, coarse_diag, coarse_vals, csmooth_diag, csmooth_vals,
    remote_row, remote_vals, interp_row, interp_vals,
):
    def rows(array):
        return array.reshape(array.shape[0], -1, BLK)

    cap = send_cell.shape[-1]
    ki = remote_row.shape[0]
    def in_hbm(array):
        return pltpu.with_memory_space_constraint(array, pltpu.HBM)

    operands = (
        rhs, diag, smoother_center, smoother_faces,
        send_count,
        send_cell.reshape(8, cap), rows(restrict_col), rows(restrict_vals),
        rows(coarse_col), coarse_diag.reshape(-1, BLK), rows(coarse_vals),
        csmooth_diag.reshape(-1, BLK), rows(csmooth_vals),
        remote_row.reshape(ki, 8, cap), remote_vals.reshape(ki, 8, cap),
        interp_row, interp_vals,
    )
    shapes = {
        "rhs": rhs.shape, "send_cell": (8, cap), "restrict_col": operands[6].shape,
        "coarse_col": operands[8].shape, "interp_row": interp_row.shape,
    }
    sizes = (lax.axis_size("gx"), lax.axis_size("gy"))
    operands = [in_hbm(x) for x in operands]
    return write_out(*make_kernel(sizes, shapes)(*operands))


def solution(mesh):
    fine = P("gx", "gy", None)
    listed = P(None, "gx", "gy", None)
    placed = (
        fine, fine, fine, listed, fine, P("gx", "gy", None, None), listed, listed,
        listed, fine, listed, fine, listed,
        P(None, "gx", "gy", None, None), P(None, "gx", "gy", None, None),
        listed, listed,
    )
    return jax.shard_map(
        body, mesh=mesh, in_specs=placed, out_specs=(fine, fine), check_vma=False
    )
```

```python
import jax
import jax.numpy as jnp
from jax import lax
from jax.experimental import pallas as pl
from jax.experimental.pallas import tpu as pltpu
from jax.sharding import PartitionSpec as P

BLK = 128
OFFSETS = ((-1, -1), (-1, 0), (-1, 1), (0, -1), (0, 1), (1, -1), (1, 0), (1, 1))
SIDES = ((-1, 0), (1, 0), (0, -1), (0, 1))
CORNERS = (0, 2, 5, 7)
MESH_ID = pl.DeviceIdType.MESH


def split_two(table):
    high = table.astype(jnp.bfloat16)
    low = (table - high.astype(jnp.float32)).astype(jnp.bfloat16)
    return jnp.concatenate([high, low], axis=1)


def one_hot(base, width):
    ids = lax.broadcasted_iota(jnp.int32, (base.shape[0], width), 1)
    return jnp.where(ids == base, 1.0, 0.0).astype(jnp.bfloat16)


def pick(index, base, table_two):
    return pick_hot(index, one_hot(base, table_two.shape[0]), table_two)


def pick_hot(index, hot, table_two):
    both = jnp.dot(hot, table_two, preferred_element_type=jnp.float32)
    rows = both[:, :BLK] + both[:, BLK:]
    return jnp.take_along_axis(rows, index & (BLK - 1), axis=1, mode="promise_in_bounds")


def make_kernel(sizes, shapes):
    na, nb = sizes
    cx, cy, nz = shapes["rhs"]
    zblocks = nz // BLK
    cells = cx * cy
    fine_rows = cells * zblocks
    cap = shapes["send_cell"][1]
    slots = cap // BLK
    kr, crows, _ = shapes["restrict_col"]
    ka = shapes["coarse_col"][0]
    ki = shapes["interp_row"][0]
    rim_rows = 8

    def fine_place(block):
        return (block % zblocks) * cells + block // zblocks

    def kernel(
        rhs_h, diag_h, center_h, faces_h, count_h, cell_h, rcol_h, rval_h, ccol_h,
        cdiag_h, cval_h, mdiag_h, mval_h, rrow_h, rrval_h, irow_h, ival_h,
        sol_ref, res_ref,
        hot_back, hot_spread, turned, count, counts, field, yrecv, diag, center, faces, edges, cell, rcol, rval, ccol, cdiag, cval,
        mdiag, mval, rrow, rrval, irow, ival, resid, fine_two, choose, sent, received,
        back, returned, coarse, rim, spread, partial,
        first_out, first_in, pre_out, pre_in, last_out, last_in, tip_out, tip_in, edges_in,
        ends_out, ends_in, in_sem, first_send, first_recv, pre_send, pre_recv, last_send, last_recv,
        tip_send, tip_recv, edges_send, edges_recv,
        slot_send, slot_recv, back_send, back_recv, rim_send, rim_recv,
    ):
        a = lax.axis_index("gx")
        b = lax.axis_index("gy")

        loads = [
            (rhs_h, field.at[0, pl.ds(1, cx)]), (center_h, center), (faces_h, faces),
            (center_h.at[0], edges.at[0, 0]), (center_h.at[cx - 1], edges.at[1, 0]),
            (center_h.at[:, 0, :], edges.at[2, 0]), (center_h.at[:, cy - 1, :], edges.at[3, 0]),
            (faces_h.at[pl.ds(2, 4), 0], edges.at[0, pl.ds(1, 4)]),
            (faces_h.at[pl.ds(2, 4), cx - 1], edges.at[1, pl.ds(1, 4)]),
            (faces_h.at[pl.ds(0, 2), :, 0, :], edges.at[2, pl.ds(1, 2)]),
            (faces_h.at[pl.ds(4, 2), :, 0, :], edges.at[2, pl.ds(3, 2)]),
            (faces_h.at[pl.ds(0, 2), :, cy - 1, :], edges.at[3, pl.ds(1, 2)]),
            (faces_h.at[pl.ds(4, 2), :, cy - 1, :], edges.at[3, pl.ds(3, 2)]),
            (diag_h, diag), (cell_h, cell), (count_h, count), (rcol_h, rcol), (rval_h, rval),
            (ccol_h, ccol), (mdiag_h, mdiag), (mval_h, mval), (cdiag_h, cdiag),
            (cval_h, cval), (rrow_h, rrow), (rrval_h, rrval), (irow_h, irow),
            (ival_h, ival),
        ]
        loads = [
            pltpu.make_async_copy(source, target, in_sem.at[n])
            for n, (source, target) in enumerate(loads)
        ]

        def there(step):
            dx, dy = step
            checks = []
            if dx < 0:
                checks.append(a > 0)
            if dx > 0:
                checks.append(a < na - 1)
            if dy < 0:
                checks.append(b > 0)
            if dy > 0:
                checks.append(b < nb - 1)
            out = checks[0]
            for check in checks[1:]:
                out = jnp.logical_and(out, check)
            return out

        exists = [there(step) for step in OFFSETS]
        side_exists = [there(step) for step in SIDES]

        barrier = pltpu.get_barrier_semaphore()
        total = jnp.int32(0)
        for d, (dx, dy) in enumerate(OFFSETS):
            @pl.when(exists[d])
            def _():
                pl.semaphore_signal(
                    barrier, inc=1, device_id=(a + dx, b + dy), device_id_type=MESH_ID
                )
            total = total + exists[d].astype(jnp.int32)

        for load in loads[:3]:
            load.start()

        def item(cond, step, src, there_ref, here_ref, send, there_sem, here_sem):
            target = (a + step[0], b + step[1])

            def copy():
                return pltpu.make_async_remote_copy(
                    src_ref=src, dst_ref=there_ref, send_sem=send, recv_sem=there_sem,
                    device_id=target, device_id_type=MESH_ID,
                )

            def arrival():
                return pltpu.make_async_remote_copy(
                    src_ref=here_ref, dst_ref=here_ref, send_sem=send, recv_sem=here_sem,
                    device_id=target, device_id_type=MESH_ID,
                )

            return cond, copy, arrival

        def side_items(out, into, send, recv):
            return [
                item(
                    side_exists[s], SIDES[s], out(s), into(s ^ 1), into(s),
                    send(s), recv(s ^ 1), recv(s),
                )
                for s in (2, 3, 0, 1)
            ]

        def corner_items(out, into, send, recv):
            return [
                item(
                    exists[CORNERS[c]], OFFSETS[CORNERS[c]], out.at[c], into.at[3 - c],
                    into.at[c], send.at[c], recv.at[3 - c], recv.at[c],
                )
                for c in range(4)
            ]

        first_items = corner_items(pre_out, pre_in, pre_send, pre_recv) + side_items(
            lambda s: first_out.at[s], lambda s: first_in.at[s],
            lambda s: first_send.at[s], lambda s: first_recv.at[s],
        )
        part = 8 * zblocks
        early_items = side_items(
            lambda s: last_out.at[s, pl.ds(0, part)], lambda s: last_in.at[s, pl.ds(0, part)],
            lambda s: last_send.at[0, s], lambda s: last_recv.at[0, s],
        )
        last_items = corner_items(tip_out, tip_in, tip_send, tip_recv) + side_items(
            lambda s: last_out.at[s, pl.ds(part, 2 * part)],
            lambda s: last_in.at[s, pl.ds(part, 2 * part)],
            lambda s: last_send.at[1, s], lambda s: last_recv.at[1, s],
        )

        def edge_items(t):
            if t == 3:
                return side_items(
                    lambda s: ends_out.at[s], lambda s: ends_in.at[s],
                    lambda s: edges_send.at[t, s], lambda s: edges_recv.at[t, s],
                )
            low, size = ((0, 2), (2, 2), (4, 1))[t]
            items = side_items(
                lambda s: edges.at[s, pl.ds(low, size)],
                lambda s: edges_in.at[s, pl.ds(low, size)],
                lambda s: edges_send.at[t, s], lambda s: edges_recv.at[t, s],
            )[0:2]
            if t == 1:
                items = items + side_items(
                    lambda s: edges.at[s], lambda s: edges_in.at[s],
                    lambda s: edges_send.at[t, s], lambda s: edges_recv.at[t, s],
                )[2:4]
            return items

        def start_items(items):
            for cond, copy, _ in items:
                @pl.when(cond)
                def _():
                    copy().start()

        def wait_items(items):
            for cond, _, arrival in items:
                @pl.when(cond)
                def _():
                    arrival().wait_recv()

        def finish_items(items):
            for cond, copy, _ in items:
                @pl.when(cond)
                def _():
                    copy().wait_send()

        def eight_copy(src, dst, send_sem, recv_sem, d):
            dx, dy = OFFSETS[d]
            return pltpu.make_async_remote_copy(
                src_ref=src(d), dst_ref=dst(7 - d), send_sem=send_sem(d),
                recv_sem=recv_sem(7 - d),
                device_id=(a + dx, b + dy), device_id_type=MESH_ID,
            )

        def eight_arrival(dst, send_sem, recv_sem, d):
            dx, dy = OFFSETS[d]
            return pltpu.make_async_remote_copy(
                src_ref=dst(d), dst_ref=dst(d), send_sem=send_sem(d), recv_sem=recv_sem(d),
                device_id=(a + dx, b + dy), device_id_type=MESH_ID,
            )

        slot_plan = (
            lambda d: sent.at[d], lambda d: received.at[d],
            lambda d: slot_send.at[d], lambda d: slot_recv.at[d],
        )
        back_plan = (
            lambda d: back.at[d], lambda d: returned.at[d],
            lambda d: back_send.at[d], lambda d: back_recv.at[d],
        )

        def rim_plan(t):
            return (
                lambda d: coarse.at[t, pl.ds(0, rim_rows)], lambda d: rim.at[t, d],
                lambda d: rim_send.at[t, d], lambda d: rim_recv.at[t, d],
            )

        def finish_eight(plan):
            for d in range(8):
                @pl.when(exists[d])
                def _():
                    eight_copy(*plan, d).wait_send()

        def start_eight(plan):
            for d in (0, 2, 5, 7, 3, 4, 1, 6):
                @pl.when(exists[d])
                def _():
                    eight_copy(*plan, d).start()

        def wait_eight(plan):
            for d in range(8):
                @pl.when(exists[d])
                def _():
                    eight_arrival(*plan[1:], d).wait_recv()

        row_ids = lax.broadcasted_iota(jnp.int32, (cy, nz), 0)
        lane_ids = lax.broadcasted_iota(jnp.int32, (cy, nz), 1)

        zeros = jnp.zeros((cy, nz), jnp.float32)

        def beside(t, i):
            centre = field[t, i + 1]
            return centre, [
                field[t, i] if i > 0 else zeros,
                field[t, i + 2] if i < cx - 1 else zeros,
                jnp.where(row_ids == 0, 0.0, pltpu.roll(centre, 1, 0)),
                jnp.where(row_ids == cy - 1, 0.0, pltpu.roll(centre, cy - 1, 0)),
                jnp.where(lane_ids == 0, 0.0, pltpu.roll(centre, 1, 1)),
                jnp.where(lane_ids == nz - 1, 0.0, pltpu.roll(centre, nz - 1, 1)),
            ]

        def sides(t, i):
            out = [
                jnp.where(row_ids == 0, jnp.broadcast_to(yrecv[t, 0, i:i + 1, :], (cy, nz)), 0.0),
                jnp.where(row_ids == cy - 1, jnp.broadcast_to(yrecv[t, 1, i:i + 1, :], (cy, nz)), 0.0),
            ]
            return [
                field[t, 0] if i == 0 else None,
                field[t, cx + 1] if i == cx - 1 else None,
            ] + out

        def residual_inside(t):
            for i in range(cx):
                centre, near = beside(t, i)
                sums = near[0]
                for one in near[1:]:
                    sums = sums + one
                partial[i] = field[0, i + 1] - ((6.0 + diag[i]) * centre - sums)

        def residual_row(t, i):
            out = partial[i]
            for one in sides(t, i):
                if one is not None:
                    out = out + one
            return out

        def smoother_inside(t, base):
            for i in range(cx):
                centre, near = beside(t, i)
                out = center[i] * centre
                for q in range(6):
                    out = out + faces[q, i] * near[q]
                partial[i] = out if base is None else field[base, i + 1] + out

        def smoother_row(t, i):
            out = partial[i]
            for q, one in enumerate(sides(t, i)):
                if one is not None:
                    out = out + faces[q, i] * one
            return out

        def put_edges(out, n, i, value):
            base = n * zblocks * 8
            for z in range(zblocks):
                part = value[:, z * BLK:(z + 1) * BLK]
                row = base + z * 8
                if i == 0:
                    out[0, row:row + 8, :] = part
                if i == cx - 1:
                    out[1, row:row + 8, :] = part
                out[2, row + i:row + i + 1, :] = part[0:1]
                out[3, row + i:row + i + 1, :] = part[cy - 1:cy]

        def layer(ref, s, n):
            base = n * zblocks * 8
            return jnp.concatenate(
                [ref[s, base + 8 * z:base + 8 * z + 8, :] for z in range(zblocks)], axis=1
            )

        def column(ref, c, low, step=1):
            return jnp.concatenate(
                [ref[c, low + z * step:low + z * step + 1, :] for z in range(zblocks)], axis=1
            )

        def put_column(ref, c, low, value):
            for z in range(zblocks):
                ref[c, low + z:low + z + 1, :] = value[:, z * BLK:(z + 1) * BLK]

        def corner_cell(c):
            dx, dy = OFFSETS[CORNERS[c]]
            return (0 if dx < 0 else cx - 1), (0 if dy < 0 else cy - 1), -dx, -dy

        ends = [(0, 1), (2, 3), (0, 2), (1, 3)]
        first_row, last_row = row_ids == 0, row_ids == cy - 1

        def at_ends(low, high):
            wide = (cy, nz)
            return jnp.where(
                first_row, jnp.broadcast_to(low, wide),
                jnp.where(last_row, jnp.broadcast_to(high, wide), 0.0),
            )

        for load in loads[0:3]:
            load.wait()
        for load in loads[3:]:
            load.start()
        smoother_inside(0, None)
        for i in range(cx):
            put_edges(first_out, 0, i, field[0, i + 1])
            put_edges(first_out, 1, i, partial[i])
        for c in range(4):
            i, j, _, _ = corner_cell(c)
            put_column(pre_out, c, 0, field[0, i + 1][j:j + 1])
        end_row = 3 * zblocks * 8
        face_rows = 2 * zblocks * 8
        for z in range(zblocks):
            p = z * BLK
            row = face_rows + z * 8
            first_out[0, row:row + 8, :] = faces[0, 0, :, p:p + BLK]
            first_out[1, row:row + 8, :] = faces[1, cx - 1, :, p:p + BLK]
            for i in range(cx):
                first_out[2, row + i:row + i + 1, :] = faces[2, i, 0:1, p:p + BLK]
                first_out[3, row + i:row + i + 1, :] = faces[3, i, cy - 1:cy, p:p + BLK]
            for s in range(4):
                place = (0 if s % 2 == 0 else (cx if s < 2 else cy) - 1)
                if s < 2:
                    at_low = faces[2, place, 0:1, p:p + BLK]
                    at_high = faces[3, place, cy - 1:cy, p:p + BLK]
                else:
                    at_low = faces[0, 0, place:place + 1, p:p + BLK]
                    at_high = faces[1, cx - 1, place:place + 1, p:p + BLK]
                first_out[s, end_row + z:end_row + z + 1, :] = at_low
                row_high = end_row + zblocks + z
                first_out[s, row_high:row_high + 1, :] = at_high
        pl.semaphore_wait(barrier, total)
        start_items(first_items)
        for s in range(4):
            @pl.when(jnp.logical_not(side_exists[s]))
            def _():
                first_in[s] = jnp.zeros(first_in.shape[1:], jnp.float32)
                last_in[s] = jnp.zeros(last_in.shape[1:], jnp.float32)
                edges_in[s] = jnp.zeros(edges_in.shape[1:], jnp.float32)
                ends_in[s] = jnp.zeros(ends_in.shape[1:], jnp.float32)
        for c in range(4):
            @pl.when(jnp.logical_not(exists[CORNERS[c]]))
            def _():
                pre_in[c] = jnp.zeros(pre_in.shape[1:], jnp.float32)
                tip_in[c] = jnp.zeros(tip_in.shape[1:], jnp.float32)
        for d in range(8):
            @pl.when(jnp.logical_not(exists[d]))
            def _():
                received[d] = jnp.zeros((slots, BLK), jnp.float32)
                returned[d] = jnp.zeros((slots, BLK), jnp.float32)
                for t in range(3):
                    rim[t, d] = jnp.zeros((rim_rows, BLK), jnp.float32)

        edge_loads, loads = loads[3:13], loads[12:]
        for load in loads[1:4]:
            load.wait()
        slot_rows = lax.broadcasted_iota(jnp.int32, (8, BLK), 0)
        value = jnp.zeros((8, BLK), jnp.int32)
        for d in range(8):
            value = jnp.where(slot_rows == d, count[0, 0, d], value)
        counts[...] = value

        cell_index = jnp.concatenate(
            [cell[:, s * BLK:(s + 1) * BLK] for s in range(slots)], axis=0
        )
        cell_base = fine_place(cell_index[:, 0:1] // BLK)
        across = jnp.transpose(
            jnp.broadcast_to(cell_base, (8 * slots, BLK)).astype(jnp.float32)
        )[0:1].astype(jnp.int32)
        fine_ids = lax.broadcasted_iota(jnp.int32, (fine_rows, 8 * slots), 0)
        choose[...] = jnp.where(fine_ids == across, 1.0, 0.0).astype(jnp.bfloat16)
        hot_slot = one_hot(cell_base, fine_rows)

        for load in loads[4:] + edge_loads:
            load.wait()
        group = 8 if slots % 8 == 0 else 1
        batch = group * ki * 8

        def back_index(c):
            parts = [(c * group + g) * BLK for g in range(group)]
            return jnp.concatenate(
                [rrow[:, :, p:p + BLK].reshape(ki * 8, BLK) for p in parts], axis=0
            )

        for c in range(slots // group):
            hot_back[c * batch:(c + 1) * batch] = one_hot(back_index(c)[:, 0:1] // BLK, crows)

        for s in range(4):
            place = (0 if s % 2 == 0 else (cx if s < 2 else cy) - 1)
            for z in range(zblocks):
                p = z * BLK
                if s < 2:
                    at_low = faces[s ^ 1, place, 0:1, p:p + BLK]
                    at_high = faces[s ^ 1, place, cy - 1:cy, p:p + BLK]
                else:
                    at_low = faces[s ^ 1, 0, place:place + 1, p:p + BLK]
                    at_high = faces[s ^ 1, cx - 1, place:place + 1, p:p + BLK]
                ends_out[s, z:z + 1, :] = at_low
                ends_out[s, zblocks + z:zblocks + z + 1, :] = at_high
        low_ids = lax.broadcasted_iota(jnp.int32, (32, BLK), 0)

        def scatter_some(s, carry):
            lower = cell[:, pl.ds(pl.multiple_of(s * BLK, BLK), BLK)] & 31
            hot_spread[s] = jnp.concatenate(
                [
                    jnp.where(jnp.broadcast_to(lower[d:d + 1], (32, BLK)) == low_ids, 1.0, 0.0)
                    for d in range(8)
                ],
                axis=0,
            ).astype(jnp.bfloat16)
            return carry

        lax.fori_loop(0, slots, scatter_some, 0, unroll=4)
        wait_items(first_items)

        def set_ghost(t, s, value):
            if s < 2:
                field[t, 0 if s == 0 else cx + 1] = value
            else:
                yrecv[t, s - 2] = value

        for s in range(4):
            set_ghost(0, s, layer(first_in, s, 0))
            low, high = ends[s]
            set_ghost(1, s, (
                layer(first_in, s, 1) + layer(first_in, s, 2) * layer(first_out, s, 0)
                + at_ends(
                    column(first_in, s, end_row) * column(pre_in, low, 0),
                    column(first_in, s, end_row + zblocks) * column(pre_in, high, 0),
                )
            ))
        for i in range(cx):
            field[1, i + 1] = smoother_row(0, i)
        residual_inside(1)
        for i in range(cx):
            resid[i] = residual_row(1, i)
        table = jnp.concatenate(
            [resid[:, :, z * BLK:(z + 1) * BLK].reshape(cells, BLK) for z in range(zblocks)],
            axis=0,
        )
        fine_two[...] = split_two(table)

        picked = pick_hot(cell_index, hot_slot, fine_two[...])
        lanes = lax.broadcasted_iota(jnp.int32, (8, BLK), 1)
        slot_ids = lax.broadcasted_iota(jnp.int32, (slots, 8, BLK), 0) * BLK + lanes[None]
        values = jnp.where(
            slot_ids < counts[...][None], picked.reshape(slots, 8, BLK), 0.0
        )
        sent[...] = jnp.swapaxes(values, 0, 1)
        start_eight(slot_plan)

        step = 9 if kr % 9 == 0 else 1

        def restrict_some(c, acc):
            index = rcol[pl.ds(c * step, step)].reshape(step * crows, BLK)
            block = index[:, 0:1] // BLK
            base = jnp.where(block < fine_rows, fine_place(block), -1)
            got = pick(index, base, fine_two[...]).reshape(step, crows, BLK)
            return acc + jnp.sum(got * rval[pl.ds(c * step, step)], axis=0)

        rc = lax.fori_loop(
            0, kr // step, restrict_some, jnp.zeros((crows, BLK), jnp.float32)
        )
        far_index = rcol[:, 0:rim_rows, :].reshape(kr * rim_rows, BLK)
        hot_far = one_hot(far_index[:, 0:1] // BLK - fine_rows, 8 * slots)
        own_index = ccol[...].reshape(ka * crows, BLK)
        hot_own = one_hot(own_index[:, 0:1] // BLK, crows)
        rim_index = ccol[:, 0:rim_rows, :].reshape(ka * rim_rows, BLK)
        hot_rim = one_hot(rim_index[:, 0:1] // BLK - crows, 8 * rim_rows)
        wait_eight(slot_plan)
        received_two = split_two(received[...].reshape(8 * slots, BLK))
        got = pick_hot(far_index, hot_far, received_two)
        more = jnp.sum(
            got.reshape(kr, rim_rows, BLK) * rval[:, 0:rim_rows, :], axis=0
        )
        rc = jnp.concatenate([rc[:rim_rows] + more, rc[rim_rows:]], axis=0)

        def coarse_apply(t, vector, diagonal, values):
            coarse[t] = vector
            start_eight(rim_plan(t))
            start_items(edge_items(t))
            if t == 2:
                start_items(edge_items(3))
            got = pick_hot(own_index, hot_own, split_two(vector))
            own = diagonal[...] * vector + jnp.sum(
                got.reshape(ka, crows, BLK) * values[...], axis=0
            )
            wait_eight(rim_plan(t))
            got = pick_hot(
                rim_index, hot_rim, split_two(rim[t].reshape(8 * rim_rows, BLK))
            )
            more = jnp.sum(
                got.reshape(ka, rim_rows, BLK) * values[:, 0:rim_rows, :], axis=0
            )
            return jnp.concatenate([own[:rim_rows] + more, own[rim_rows:]], axis=0)

        xc1 = coarse_apply(0, rc, mdiag, mval)
        rc2 = rc - coarse_apply(1, xc1, cdiag, cval)
        xc2 = xc1 + coarse_apply(2, rc2, mdiag, mval)
        coarse_two = split_two(xc2)

        for c in range(slots // group):
            parts = [(c * group + g) * BLK for g in range(group)]
            got = pick_hot(
                back_index(c), hot_back[c * batch:(c + 1) * batch], coarse_two
            )
            values = []
            for g, p in enumerate(parts):
                mine = got[g * ki * 8:(g + 1) * ki * 8].reshape(ki, 8, BLK)
                values.append(jnp.sum(mine * rrval[:, :, p:p + BLK], axis=0))
            back[:, c * group:(c + 1) * group, :] = jnp.swapaxes(jnp.stack(values), 0, 1)
        start_eight(back_plan)

        for z in range(zblocks):
            p = z * BLK
            index = irow[:, :, :, p:p + BLK].reshape(ki * cells, BLK)
            got = pick(index, index[:, 0:1] // BLK, coarse_two)
            got = got.reshape(ki, cx, cy, BLK) * ival[:, :, :, p:p + BLK]
            field[2, 1:cx + 1, :, p:p + BLK] = (
                field[1, 1:cx + 1, :, p:p + BLK] + jnp.sum(got, axis=0)
            )
        finish_items(first_items)
        finish_eight(slot_plan)
        for t in range(3):
            finish_eight(rim_plan(t))
        wait_eight(back_plan)

        in_place = lanes // 32 == slot_rows % 4

        def spread_some(s, carry):
            p = pl.multiple_of(s * BLK, BLK)
            values = jnp.where(lanes + p < counts[...], turned[s], 0.0)
            high = values.astype(jnp.bfloat16).astype(jnp.float32)
            low = values - high
            turn = ((cell[:, pl.ds(p, BLK)] & (BLK - 1)) // 32 - slot_rows) & 3
            left_side = jnp.concatenate(
                [jnp.where(turn == h, part, 0.0) for part in (high, low) for h in range(4)],
                axis=0,
            ).astype(jnp.bfloat16)
            both = lax.dot_general(
                left_side, hot_spread[s], (((1,), (1,)), ((), ())),
                preferred_element_type=jnp.float32,
            )
            both = both[:32] + both[32:]
            out = jnp.zeros((8, BLK), jnp.float32)
            for h in range(4):
                near = both[8 * h:8 * h + 8]
                near = jnp.where(slot_rows < 4, near[:, :BLK], near[:, BLK:])
                near = jnp.where(in_place, near, 0.0)
                out = out + (pltpu.roll(near, 32 * h, 1) if h else near)
            spread[pl.ds(pl.multiple_of(s * 8, 8), 8)] = out
            return carry

        turned[...] = jnp.swapaxes(returned[...], 0, 1)
        lax.fori_loop(0, slots, spread_some, 0, unroll=32)
        both = jnp.dot(
            choose[...], split_two(spread[...]), preferred_element_type=jnp.float32
        )
        added = both[:, :BLK] + both[:, BLK:]
        for z in range(zblocks):
            p = z * BLK
            field[2, 1:cx + 1, :, p:p + BLK] = (
                field[2, 1:cx + 1, :, p:p + BLK]
                + added[z * cells:(z + 1) * cells].reshape(cx, cy, BLK)
            )
        for i in range(cx):
            put_edges(last_out, 0, i, field[2, i + 1])
        start_items(early_items)
        residual_inside(2)
        for i in range(cx):
            field[3, i + 1] = partial[i]
        smoother_inside(3, 2)
        for i in range(cx):
            put_edges(last_out, 1, i, field[3, i + 1])
            put_edges(last_out, 2, i, partial[i])
        for c in range(4):
            i, j, di, dj = corner_cell(c)
            put_column(tip_out, c, 0, field[2, i + 1][j:j + 1])
            put_column(tip_out, c, zblocks, field[2, i + 1][j + dj:j + dj + 1])
            put_column(tip_out, c, 2 * zblocks, field[2, i + 1 + di][j:j + 1])
            put_column(tip_out, c, 3 * zblocks, field[3, i + 1][j:j + 1])
        start_items(last_items)
        finish_eight(back_plan)
        for t in range(4):
            finish_items(edge_items(t))
            wait_items(edge_items(t))
        wait_items(early_items)
        wait_items(last_items)

        beyond = [layer(last_in, s, 0) for s in range(4)]
        for s in range(4):
            set_ghost(2, s, beyond[s])
        corner_resid = []
        for c in range(4):
            i, j, _, _ = corner_cell(c)
            sx, sy = (0 if i == 0 else 1), (2 if j == 0 else 3)
            value = (
                column(tip_in, c, 3 * zblocks) + beyond[sx][j:j + 1] + beyond[sy][i:i + 1]
            )
            corner_resid.append(jnp.where(exists[CORNERS[c]], value, 0.0))

        for s in range(4):
            low, high = ends[s]
            place = 0 if s % 2 == 0 else cy - 1
            low_side, high_side = (2, 3) if s < 2 else (0, 1)
            change = layer(last_out, s, 0) + at_ends(
                column(tip_in, low, 0), column(tip_in, high, 0)
            )
            beyond_resid = jnp.where(
                side_exists[s], layer(last_in, s, 1) + change, 0.0
            )
            set_ghost(3, s, beyond_resid)
            own_resid = layer(last_out, s, 1) + beyond[s] + at_ends(
                beyond[low_side][place:place + 1], beyond[high_side][place:place + 1]
            )
            wide = (cy, nz)
            before = jnp.where(
                first_row, jnp.broadcast_to(corner_resid[low], wide), pltpu.roll(change, 1, 0)
            )
            after = jnp.where(
                last_row, jnp.broadcast_to(corner_resid[high], wide),
                pltpu.roll(change, cy - 1, 0),
            )
            column_low = zblocks if s >= 2 else 2 * zblocks
            second = at_ends(
                column(ends_in, s, 0) * column(tip_in, low, column_low),
                column(ends_in, s, zblocks) * column(tip_in, high, column_low),
            )
            set_ghost(4, s, (
                layer(last_in, s, 2)
                + edges_in[s, 0] * change
                + edges_in[s, 1] * before
                + edges_in[s, 2] * after
                + layer(first_in, s, 2) * own_resid
                + second
                + edges_in[s, 3] * jnp.where(lane_ids == 0, 0.0, pltpu.roll(change, 1, 1))
                + edges_in[s, 4] * jnp.where(lane_ids == nz - 1, 0.0, pltpu.roll(change, nz - 1, 1))
            ))
        for i in range(cx):
            partial[i] = field[3, i + 1]
        for i in range(cx):
            field[3, i + 1] = residual_row(2, i)
        smoother_inside(3, 2)
        for i in range(cx):
            value = smoother_row(3, i)
            field[4, i + 1] = value
            sol_ref[i] = value
        residual_inside(4)
        for i in range(cx):
            res_ref[i] = residual_row(4, i)

        finish_items(early_items)
        finish_items(last_items)

    f32, i32, bf16 = jnp.float32, jnp.int32, jnp.bfloat16
    vm = pltpu.VMEM
    dma = pltpu.SemaphoreType.DMA
    scratch = [
        vm((ki * 8 * slots, crows), bf16), vm((slots, 256, BLK), bf16), vm((slots, 8, BLK), f32),
        pltpu.SMEM((1, 1, 8), i32), vm((8, BLK), i32),
        vm((5, cx + 2, cy, nz), f32), vm((5, 2, cx, nz), f32),
        vm((cx, cy, nz), f32), vm((cx, cy, nz), f32), vm((6, cx, cy, nz), f32),
        vm((4, 5, 8, nz), f32),
        vm((8, cap), i32), vm((kr, crows, BLK), i32), vm((kr, crows, BLK), f32),
        vm((ka, crows, BLK), i32), vm((crows, BLK), f32), vm((ka, crows, BLK), f32),
        vm((crows, BLK), f32), vm((ka, crows, BLK), f32),
        vm((ki, 8, cap), i32), vm((ki, 8, cap), f32),
        vm((ki, cx, cy, nz), i32), vm((ki, cx, cy, nz), f32),
        vm((cx, cy, nz), f32), vm((fine_rows, 2 * BLK), bf16),
        vm((fine_rows, 8 * slots), bf16),
        vm((8, slots, BLK), f32), vm((8, slots, BLK), f32),
        vm((8, slots, BLK), f32), vm((8, slots, BLK), f32),
        vm((3, crows, BLK), f32), vm((3, 8, rim_rows, BLK), f32),
        vm((8 * slots, BLK), f32), vm((cx, cy, nz), f32),
        vm((4, (3 * 8 + 2) * zblocks, BLK), f32), vm((4, (3 * 8 + 2) * zblocks, BLK), f32),
        vm((4, zblocks, BLK), f32), vm((4, zblocks, BLK), f32),
        vm((4, 3 * 8 * zblocks, BLK), f32), vm((4, 3 * 8 * zblocks, BLK), f32),
        vm((4, 4 * zblocks, BLK), f32), vm((4, 4 * zblocks, BLK), f32),
        vm((4, 5, 8, nz), f32),
        vm((4, 2 * zblocks, BLK), f32), vm((4, 2 * zblocks, BLK), f32),
        dma((27,)), dma((4,)), dma((4,)), dma((4,)), dma((4,)), dma((2, 4)), dma((2, 4)),
        dma((4,)), dma((4,)), dma((4, 4)), dma((4, 4)),
        dma((8,)), dma((8,)), dma((8,)), dma((8,)),
        dma((3, 8)), dma((3, 8)),
    ]
    whole = pl.BlockSpec(memory_space=pltpu.VMEM)
    in_hbm = pl.BlockSpec(memory_space=pltpu.HBM)
    return pl.pallas_call(
        kernel,
        out_shape=(
            jax.ShapeDtypeStruct((cx, cy, nz), f32),
            jax.ShapeDtypeStruct((cx, cy, nz), f32),
        ),
        in_specs=[in_hbm] * 17,
        out_specs=(whole, whole),
        scratch_shapes=scratch,
        compiler_params=pltpu.CompilerParams(
            collective_id=0, has_side_effects=True, vmem_limit_bytes=40 * 1024 * 1024
        ),
        name="vcycle",
    )


def write_out(first, second):
    def kernel(first_ref, second_ref, first_out, second_out, sem):
        copies = [
            pltpu.make_async_copy(first_ref, first_out, sem.at[0]),
            pltpu.make_async_copy(second_ref, second_out, sem.at[1]),
        ]
        for copy in copies:
            copy.start()
        for copy in copies:
            copy.wait()

    return pl.pallas_call(
        kernel,
        out_shape=(
            jax.ShapeDtypeStruct(first.shape, first.dtype),
            jax.ShapeDtypeStruct(second.shape, second.dtype),
        ),
        in_specs=[pl.BlockSpec(memory_space=pltpu.VMEM)] * 2,
        out_specs=(pl.BlockSpec(memory_space=pltpu.HBM),) * 2,
        scratch_shapes=[pltpu.SemaphoreType.DMA((2,))],
        compiler_params=pltpu.CompilerParams(vmem_limit_bytes=4 * 1024 * 1024),
        name="write_out",
    )(first, second)


def body(
    rhs, diag, smoother_center, smoother_faces, send_count, send_cell, restrict_col,
    restrict_vals, coarse_col, coarse_diag, coarse_vals, csmooth_diag, csmooth_vals,
    remote_row, remote_vals, interp_row, interp_vals,
):
    def rows(array):
        return array.reshape(array.shape[0], -1, BLK)

    cap = send_cell.shape[-1]
    ki = remote_row.shape[0]
    def in_hbm(array):
        return pltpu.with_memory_space_constraint(array, pltpu.HBM)

    operands = (
        rhs, diag, smoother_center, smoother_faces,
        send_count,
        send_cell.reshape(8, cap), rows(restrict_col), rows(restrict_vals),
        rows(coarse_col), coarse_diag.reshape(-1, BLK), rows(coarse_vals),
        csmooth_diag.reshape(-1, BLK), rows(csmooth_vals),
        remote_row.reshape(ki, 8, cap), remote_vals.reshape(ki, 8, cap),
        interp_row, interp_vals,
    )
    shapes = {
        "rhs": rhs.shape, "send_cell": (8, cap), "restrict_col": operands[6].shape,
        "coarse_col": operands[8].shape, "interp_row": interp_row.shape,
    }
    sizes = (lax.axis_size("gx"), lax.axis_size("gy"))
    operands = [in_hbm(x) for x in operands]
    return write_out(*make_kernel(sizes, shapes)(*operands))


def solution(mesh):
    fine = P("gx", "gy", None)
    listed = P(None, "gx", "gy", None)
    placed = (
        fine, fine, fine, listed, fine, P("gx", "gy", None, None), listed, listed,
        listed, fine, listed, fine, listed,
        P(None, "gx", "gy", None, None), P(None, "gx", "gy", None, None),
        listed, listed,
    )
    return jax.shard_map(
        body, mesh=mesh, in_specs=placed, out_specs=(fine, fine), check_vma=False
    )
```

```python
import jax
import jax.numpy as jnp
from jax import lax
from jax.experimental import pallas as pl
from jax.experimental.pallas import tpu as pltpu
from jax.sharding import PartitionSpec as P

BLK = 128
OFFSETS = ((-1, -1), (-1, 0), (-1, 1), (0, -1), (0, 1), (1, -1), (1, 0), (1, 1))
SIDES = ((-1, 0), (1, 0), (0, -1), (0, 1))
CORNERS = (0, 2, 5, 7)
MESH_ID = pl.DeviceIdType.MESH


def split_two(table):
    high = table.astype(jnp.bfloat16)
    low = (table - high.astype(jnp.float32)).astype(jnp.bfloat16)
    return jnp.concatenate([high, low], axis=1)


def one_hot(base, width):
    ids = lax.broadcasted_iota(jnp.int32, (base.shape[0], width), 1)
    return jnp.where(ids == base, 1.0, 0.0).astype(jnp.bfloat16)


def pick(index, base, table_two):
    return pick_hot(index, one_hot(base, table_two.shape[0]), table_two)


def pick_hot(index, hot, table_two):
    both = jnp.dot(hot, table_two, preferred_element_type=jnp.float32)
    rows = both[:, :BLK] + both[:, BLK:]
    return jnp.take_along_axis(rows, index & (BLK - 1), axis=1, mode="promise_in_bounds")


def make_kernel(sizes, shapes):
    na, nb = sizes
    cx, cy, nz = shapes["rhs"]
    zblocks = nz // BLK
    cells = cx * cy
    fine_rows = cells * zblocks
    cap = shapes["send_cell"][1]
    slots = cap // BLK
    kr, crows, _ = shapes["restrict_col"]
    ka = shapes["coarse_col"][0]
    ki = shapes["interp_row"][0]
    rim_rows = 8

    def fine_place(block):
        return (block % zblocks) * cells + block // zblocks

    def kernel(
        rhs_h, diag_h, center_h, faces_h, count_h, cell_h, rcol_h, rval_h, ccol_h,
        cdiag_h, cval_h, mdiag_h, mval_h, rrow_h, rrval_h, irow_h, ival_h,
        sol_ref, res_ref,
        hot_back, hot_spread, turned, count, counts, field, yrecv, diag, center, faces, edges, cell, rcol, rval, ccol, cdiag, cval,
        mdiag, mval, rrow, rrval, irow, ival, resid, fine_two, choose, sent, received,
        back, returned, coarse, rim, spread, partial,
        first_out, first_in, pre_out, pre_in, last_out, last_in, tip_out, tip_in, edges_in,
        ends_out, ends_in, in_sem, first_send, first_recv, pre_send, pre_recv, last_send, last_recv,
        tip_send, tip_recv, edges_send, edges_recv,
        slot_send, slot_recv, back_send, back_recv, rim_send, rim_recv,
    ):
        a = lax.axis_index("gx")
        b = lax.axis_index("gy")

        loads = [
            (rhs_h, field.at[0, pl.ds(1, cx)]), (center_h, center), (faces_h, faces),
            (center_h.at[0], edges.at[0, 0]), (center_h.at[cx - 1], edges.at[1, 0]),
            (center_h.at[:, 0, :], edges.at[2, 0]), (center_h.at[:, cy - 1, :], edges.at[3, 0]),
            (faces_h.at[pl.ds(2, 4), 0], edges.at[0, pl.ds(1, 4)]),
            (faces_h.at[pl.ds(2, 4), cx - 1], edges.at[1, pl.ds(1, 4)]),
            (faces_h.at[pl.ds(0, 2), :, 0, :], edges.at[2, pl.ds(1, 2)]),
            (faces_h.at[pl.ds(4, 2), :, 0, :], edges.at[2, pl.ds(3, 2)]),
            (faces_h.at[pl.ds(0, 2), :, cy - 1, :], edges.at[3, pl.ds(1, 2)]),
            (faces_h.at[pl.ds(4, 2), :, cy - 1, :], edges.at[3, pl.ds(3, 2)]),
            (diag_h, diag), (cell_h, cell), (count_h, count), (rcol_h, rcol), (rval_h, rval),
            (ccol_h, ccol), (mdiag_h, mdiag), (mval_h, mval), (cdiag_h, cdiag),
            (cval_h, cval), (rrow_h, rrow), (rrval_h, rrval), (irow_h, irow),
            (ival_h, ival),
        ]
        loads = [
            pltpu.make_async_copy(source, target, in_sem.at[n])
            for n, (source, target) in enumerate(loads)
        ]

        def there(step):
            dx, dy = step
            checks = []
            if dx < 0:
                checks.append(a > 0)
            if dx > 0:
                checks.append(a < na - 1)
            if dy < 0:
                checks.append(b > 0)
            if dy > 0:
                checks.append(b < nb - 1)
            out = checks[0]
            for check in checks[1:]:
                out = jnp.logical_and(out, check)
            return out

        exists = [there(step) for step in OFFSETS]
        side_exists = [there(step) for step in SIDES]

        barrier = pltpu.get_barrier_semaphore()
        total = jnp.int32(0)
        for d, (dx, dy) in enumerate(OFFSETS):
            @pl.when(exists[d])
            def _():
                pl.semaphore_signal(
                    barrier, inc=1, device_id=(a + dx, b + dy), device_id_type=MESH_ID
                )
            total = total + exists[d].astype(jnp.int32)

        for load in loads:
            load.start()

        def item(cond, step, src, there_ref, here_ref, send, there_sem, here_sem):
            target = (a + step[0], b + step[1])

            def copy():
                return pltpu.make_async_remote_copy(
                    src_ref=src, dst_ref=there_ref, send_sem=send, recv_sem=there_sem,
                    device_id=target, device_id_type=MESH_ID,
                )

            def arrival():
                return pltpu.make_async_remote_copy(
                    src_ref=here_ref, dst_ref=here_ref, send_sem=send, recv_sem=here_sem,
                    device_id=target, device_id_type=MESH_ID,
                )

            return cond, copy, arrival

        def side_items(out, into, send, recv):
            return [
                item(
                    side_exists[s], SIDES[s], out(s), into(s ^ 1), into(s),
                    send(s), recv(s ^ 1), recv(s),
                )
                for s in (2, 3, 0, 1)
            ]

        def corner_items(out, into, send, recv):
            return [
                item(
                    exists[CORNERS[c]], OFFSETS[CORNERS[c]], out.at[c], into.at[3 - c],
                    into.at[c], send.at[c], recv.at[3 - c], recv.at[c],
                )
                for c in range(4)
            ]

        first_items = corner_items(pre_out, pre_in, pre_send, pre_recv) + side_items(
            lambda s: first_out.at[s], lambda s: first_in.at[s],
            lambda s: first_send.at[s], lambda s: first_recv.at[s],
        )
        part = 8 * zblocks
        early_items = side_items(
            lambda s: last_out.at[s, pl.ds(0, part)], lambda s: last_in.at[s, pl.ds(0, part)],
            lambda s: last_send.at[0, s], lambda s: last_recv.at[0, s],
        )
        last_items = corner_items(tip_out, tip_in, tip_send, tip_recv) + side_items(
            lambda s: last_out.at[s, pl.ds(part, 2 * part)],
            lambda s: last_in.at[s, pl.ds(part, 2 * part)],
            lambda s: last_send.at[1, s], lambda s: last_recv.at[1, s],
        )

        def edge_items(t):
            if t == 3:
                return side_items(
                    lambda s: ends_out.at[s], lambda s: ends_in.at[s],
                    lambda s: edges_send.at[t, s], lambda s: edges_recv.at[t, s],
                )
            low, size = ((0, 2), (2, 2), (4, 1))[t]
            items = side_items(
                lambda s: edges.at[s, pl.ds(low, size)],
                lambda s: edges_in.at[s, pl.ds(low, size)],
                lambda s: edges_send.at[t, s], lambda s: edges_recv.at[t, s],
            )[0:2]
            if t == 1:
                items = items + side_items(
                    lambda s: edges.at[s], lambda s: edges_in.at[s],
                    lambda s: edges_send.at[t, s], lambda s: edges_recv.at[t, s],
                )[2:4]
            return items

        def start_items(items):
            for cond, copy, _ in items:
                @pl.when(cond)
                def _():
                    copy().start()

        def wait_items(items):
            for cond, _, arrival in items:
                @pl.when(cond)
                def _():
                    arrival().wait_recv()

        def finish_items(items):
            for cond, copy, _ in items:
                @pl.when(cond)
                def _():
                    copy().wait_send()

        def eight_copy(src, dst, send_sem, recv_sem, d):
            dx, dy = OFFSETS[d]
            return pltpu.make_async_remote_copy(
                src_ref=src(d), dst_ref=dst(7 - d), send_sem=send_sem(d),
                recv_sem=recv_sem(7 - d),
                device_id=(a + dx, b + dy), device_id_type=MESH_ID,
            )

        def eight_arrival(dst, send_sem, recv_sem, d):
            dx, dy = OFFSETS[d]
            return pltpu.make_async_remote_copy(
                src_ref=dst(d), dst_ref=dst(d), send_sem=send_sem(d), recv_sem=recv_sem(d),
                device_id=(a + dx, b + dy), device_id_type=MESH_ID,
            )

        slot_plan = (
            lambda d: sent.at[d], lambda d: received.at[d],
            lambda d: slot_send.at[d], lambda d: slot_recv.at[d],
        )
        back_plan = (
            lambda d: back.at[d], lambda d: returned.at[d],
            lambda d: back_send.at[d], lambda d: back_recv.at[d],
        )

        def rim_plan(t):
            return (
                lambda d: coarse.at[t, pl.ds(0, rim_rows)], lambda d: rim.at[t, d],
                lambda d: rim_send.at[t, d], lambda d: rim_recv.at[t, d],
            )

        def finish_eight(plan):
            for d in range(8):
                @pl.when(exists[d])
                def _():
                    eight_copy(*plan, d).wait_send()

        def start_eight(plan):
            for d in (0, 2, 5, 7, 3, 4, 1, 6):
                @pl.when(exists[d])
                def _():
                    eight_copy(*plan, d).start()

        def wait_eight(plan):
            for d in range(8):
                @pl.when(exists[d])
                def _():
                    eight_arrival(*plan[1:], d).wait_recv()

        row_ids = lax.broadcasted_iota(jnp.int32, (cy, nz), 0)
        lane_ids = lax.broadcasted_iota(jnp.int32, (cy, nz), 1)

        zeros = jnp.zeros((cy, nz), jnp.float32)

        def beside(t, i):
            centre = field[t, i + 1]
            return centre, [
                field[t, i] if i > 0 else zeros,
                field[t, i + 2] if i < cx - 1 else zeros,
                jnp.where(row_ids == 0, 0.0, pltpu.roll(centre, 1, 0)),
                jnp.where(row_ids == cy - 1, 0.0, pltpu.roll(centre, cy - 1, 0)),
                jnp.where(lane_ids == 0, 0.0, pltpu.roll(centre, 1, 1)),
                jnp.where(lane_ids == nz - 1, 0.0, pltpu.roll(centre, nz - 1, 1)),
            ]

        def sides(t, i):
            out = [
                jnp.where(row_ids == 0, jnp.broadcast_to(yrecv[t, 0, i:i + 1, :], (cy, nz)), 0.0),
                jnp.where(row_ids == cy - 1, jnp.broadcast_to(yrecv[t, 1, i:i + 1, :], (cy, nz)), 0.0),
            ]
            return [
                field[t, 0] if i == 0 else None,
                field[t, cx + 1] if i == cx - 1 else None,
            ] + out

        def residual_inside(t):
            for i in range(cx):
                centre, near = beside(t, i)
                sums = near[0]
                for one in near[1:]:
                    sums = sums + one
                partial[i] = field[0, i + 1] - ((6.0 + diag[i]) * centre - sums)

        def residual_row(t, i):
            out = partial[i]
            for one in sides(t, i):
                if one is not None:
                    out = out + one
            return out

        def smoother_inside(t, base):
            for i in range(cx):
                centre, near = beside(t, i)
                out = center[i] * centre
                for q in range(6):
                    out = out + faces[q, i] * near[q]
                partial[i] = out if base is None else field[base, i + 1] + out

        def smoother_row(t, i):
            out = partial[i]
            for q, one in enumerate(sides(t, i)):
                if one is not None:
                    out = out + faces[q, i] * one
            return out

        def put_edges(out, n, i, value):
            base = n * zblocks * 8
            for z in range(zblocks):
                part = value[:, z * BLK:(z + 1) * BLK]
                row = base + z * 8
                if i == 0:
                    out[0, row:row + 8, :] = part
                if i == cx - 1:
                    out[1, row:row + 8, :] = part
                out[2, row + i:row + i + 1, :] = part[0:1]
                out[3, row + i:row + i + 1, :] = part[cy - 1:cy]

        def layer(ref, s, n):
            base = n * zblocks * 8
            return jnp.concatenate(
                [ref[s, base + 8 * z:base + 8 * z + 8, :] for z in range(zblocks)], axis=1
            )

        def column(ref, c, low, step=1):
            return jnp.concatenate(
                [ref[c, low + z * step:low + z * step + 1, :] for z in range(zblocks)], axis=1
            )

        def put_column(ref, c, low, value):
            for z in range(zblocks):
                ref[c, low + z:low + z + 1, :] = value[:, z * BLK:(z + 1) * BLK]

        def corner_cell(c):
            dx, dy = OFFSETS[CORNERS[c]]
            return (0 if dx < 0 else cx - 1), (0 if dy < 0 else cy - 1), -dx, -dy

        ends = [(0, 1), (2, 3), (0, 2), (1, 3)]
        first_row, last_row = row_ids == 0, row_ids == cy - 1

        def at_ends(low, high):
            wide = (cy, nz)
            return jnp.where(
                first_row, jnp.broadcast_to(low, wide),
                jnp.where(last_row, jnp.broadcast_to(high, wide), 0.0),
            )

        for load in loads[0:3]:
            load.wait()
        smoother_inside(0, None)
        for i in range(cx):
            put_edges(first_out, 0, i, field[0, i + 1])
            put_edges(first_out, 1, i, partial[i])
        for c in range(4):
            i, j, _, _ = corner_cell(c)
            put_column(pre_out, c, 0, field[0, i + 1][j:j + 1])
        end_row = 3 * zblocks * 8
        face_rows = 2 * zblocks * 8
        for z in range(zblocks):
            p = z * BLK
            row = face_rows + z * 8
            first_out[0, row:row + 8, :] = faces[0, 0, :, p:p + BLK]
            first_out[1, row:row + 8, :] = faces[1, cx - 1, :, p:p + BLK]
            for i in range(cx):
                first_out[2, row + i:row + i + 1, :] = faces[2, i, 0:1, p:p + BLK]
                first_out[3, row + i:row + i + 1, :] = faces[3, i, cy - 1:cy, p:p + BLK]
            for s in range(4):
                place = (0 if s % 2 == 0 else (cx if s < 2 else cy) - 1)
                if s < 2:
                    at_low = faces[2, place, 0:1, p:p + BLK]
                    at_high = faces[3, place, cy - 1:cy, p:p + BLK]
                else:
                    at_low = faces[0, 0, place:place + 1, p:p + BLK]
                    at_high = faces[1, cx - 1, place:place + 1, p:p + BLK]
                first_out[s, end_row + z:end_row + z + 1, :] = at_low
                row_high = end_row + zblocks + z
                first_out[s, row_high:row_high + 1, :] = at_high
        pl.semaphore_wait(barrier, total)
        start_items(first_items)
        for s in range(4):
            @pl.when(jnp.logical_not(side_exists[s]))
            def _():
                first_in[s] = jnp.zeros(first_in.shape[1:], jnp.float32)
                last_in[s] = jnp.zeros(last_in.shape[1:], jnp.float32)
                edges_in[s] = jnp.zeros(edges_in.shape[1:], jnp.float32)
                ends_in[s] = jnp.zeros(ends_in.shape[1:], jnp.float32)
        for c in range(4):
            @pl.when(jnp.logical_not(exists[CORNERS[c]]))
            def _():
                pre_in[c] = jnp.zeros(pre_in.shape[1:], jnp.float32)
                tip_in[c] = jnp.zeros(tip_in.shape[1:], jnp.float32)
        for d in range(8):
            @pl.when(jnp.logical_not(exists[d]))
            def _():
                received[d] = jnp.zeros((slots, BLK), jnp.float32)
                returned[d] = jnp.zeros((slots, BLK), jnp.float32)
                for t in range(3):
                    rim[t, d] = jnp.zeros((rim_rows, BLK), jnp.float32)

        edge_loads, loads = loads[3:13], loads[12:]
        for load in loads[1:4]:
            load.wait()
        slot_rows = lax.broadcasted_iota(jnp.int32, (8, BLK), 0)
        value = jnp.zeros((8, BLK), jnp.int32)
        for d in range(8):
            value = jnp.where(slot_rows == d, count[0, 0, d], value)
        counts[...] = value

        cell_index = jnp.concatenate(
            [cell[:, s * BLK:(s + 1) * BLK] for s in range(slots)], axis=0
        )
        cell_base = fine_place(cell_index[:, 0:1] // BLK)
        across = jnp.transpose(
            jnp.broadcast_to(cell_base, (8 * slots, BLK)).astype(jnp.float32)
        )[0:1].astype(jnp.int32)
        fine_ids = lax.broadcasted_iota(jnp.int32, (fine_rows, 8 * slots), 0)
        choose[...] = jnp.where(fine_ids == across, 1.0, 0.0).astype(jnp.bfloat16)
        hot_slot = one_hot(cell_base, fine_rows)

        for load in loads[4:] + edge_loads:
            load.wait()
        group = 8 if slots % 8 == 0 else 1
        batch = group * ki * 8

        def back_index(c):
            parts = [(c * group + g) * BLK for g in range(group)]
            return jnp.concatenate(
                [rrow[:, :, p:p + BLK].reshape(ki * 8, BLK) for p in parts], axis=0
            )

        for c in range(slots // group):
            hot_back[c * batch:(c + 1) * batch] = one_hot(back_index(c)[:, 0:1] // BLK, crows)

        for s in range(4):
            place = (0 if s % 2 == 0 else (cx if s < 2 else cy) - 1)
            for z in range(zblocks):
                p = z * BLK
                if s < 2:
                    at_low = faces[s ^ 1, place, 0:1, p:p + BLK]
                    at_high = faces[s ^ 1, place, cy - 1:cy, p:p + BLK]
                else:
                    at_low = faces[s ^ 1, 0, place:place + 1, p:p + BLK]
                    at_high = faces[s ^ 1, cx - 1, place:place + 1, p:p + BLK]
                ends_out[s, z:z + 1, :] = at_low
                ends_out[s, zblocks + z:zblocks + z + 1, :] = at_high
        low_ids = lax.broadcasted_iota(jnp.int32, (32, BLK), 0)

        def scatter_some(s, carry):
            lower = cell[:, pl.ds(pl.multiple_of(s * BLK, BLK), BLK)] & 31
            hot_spread[s] = jnp.concatenate(
                [
                    jnp.where(jnp.broadcast_to(lower[d:d + 1], (32, BLK)) == low_ids, 1.0, 0.0)
                    for d in range(8)
                ],
                axis=0,
            ).astype(jnp.bfloat16)
            return carry

        lax.fori_loop(0, slots, scatter_some, 0, unroll=4)
        wait_items(first_items)

        def set_ghost(t, s, value):
            if s < 2:
                field[t, 0 if s == 0 else cx + 1] = value
            else:
                yrecv[t, s - 2] = value

        for s in range(4):
            set_ghost(0, s, layer(first_in, s, 0))
            low, high = ends[s]
            set_ghost(1, s, (
                layer(first_in, s, 1) + layer(first_in, s, 2) * layer(first_out, s, 0)
                + at_ends(
                    column(first_in, s, end_row) * column(pre_in, low, 0),
                    column(first_in, s, end_row + zblocks) * column(pre_in, high, 0),
                )
            ))
        for i in range(cx):
            field[1, i + 1] = smoother_row(0, i)
        residual_inside(1)
        for i in range(cx):
            resid[i] = residual_row(1, i)
        table = jnp.concatenate(
            [resid[:, :, z * BLK:(z + 1) * BLK].reshape(cells, BLK) for z in range(zblocks)],
            axis=0,
        )
        fine_two[...] = split_two(table)

        picked = pick_hot(cell_index, hot_slot, fine_two[...])
        lanes = lax.broadcasted_iota(jnp.int32, (8, BLK), 1)
        slot_ids = lax.broadcasted_iota(jnp.int32, (slots, 8, BLK), 0) * BLK + lanes[None]
        values = jnp.where(
            slot_ids < counts[...][None], picked.reshape(slots, 8, BLK), 0.0
        )
        sent[...] = jnp.swapaxes(values, 0, 1)
        start_eight(slot_plan)

        step = 9 if kr % 9 == 0 else 1

        def restrict_some(c, acc):
            index = rcol[pl.ds(c * step, step)].reshape(step * crows, BLK)
            block = index[:, 0:1] // BLK
            base = jnp.where(block < fine_rows, fine_place(block), -1)
            got = pick(index, base, fine_two[...]).reshape(step, crows, BLK)
            return acc + jnp.sum(got * rval[pl.ds(c * step, step)], axis=0)

        rc = lax.fori_loop(
            0, kr // step, restrict_some, jnp.zeros((crows, BLK), jnp.float32)
        )
        far_index = rcol[:, 0:rim_rows, :].reshape(kr * rim_rows, BLK)
        hot_far = one_hot(far_index[:, 0:1] // BLK - fine_rows, 8 * slots)
        own_index = ccol[...].reshape(ka * crows, BLK)
        hot_own = one_hot(own_index[:, 0:1] // BLK, crows)
        rim_index = ccol[:, 0:rim_rows, :].reshape(ka * rim_rows, BLK)
        hot_rim = one_hot(rim_index[:, 0:1] // BLK - crows, 8 * rim_rows)
        wait_eight(slot_plan)
        received_two = split_two(received[...].reshape(8 * slots, BLK))
        got = pick_hot(far_index, hot_far, received_two)
        more = jnp.sum(
            got.reshape(kr, rim_rows, BLK) * rval[:, 0:rim_rows, :], axis=0
        )
        rc = jnp.concatenate([rc[:rim_rows] + more, rc[rim_rows:]], axis=0)

        def coarse_apply(t, vector, diagonal, values):
            coarse[t] = vector
            start_eight(rim_plan(t))
            start_items(edge_items(t))
            if t == 2:
                start_items(edge_items(3))
            got = pick_hot(own_index, hot_own, split_two(vector))
            own = diagonal[...] * vector + jnp.sum(
                got.reshape(ka, crows, BLK) * values[...], axis=0
            )
            wait_eight(rim_plan(t))
            got = pick_hot(
                rim_index, hot_rim, split_two(rim[t].reshape(8 * rim_rows, BLK))
            )
            more = jnp.sum(
                got.reshape(ka, rim_rows, BLK) * values[:, 0:rim_rows, :], axis=0
            )
            return jnp.concatenate([own[:rim_rows] + more, own[rim_rows:]], axis=0)

        xc1 = coarse_apply(0, rc, mdiag, mval)
        rc2 = rc - coarse_apply(1, xc1, cdiag, cval)
        xc2 = xc1 + coarse_apply(2, rc2, mdiag, mval)
        coarse_two = split_two(xc2)

        for c in range(slots // group):
            parts = [(c * group + g) * BLK for g in range(group)]
            got = pick_hot(
                back_index(c), hot_back[c * batch:(c + 1) * batch], coarse_two
            )
            values = []
            for g, p in enumerate(parts):
                mine = got[g * ki * 8:(g + 1) * ki * 8].reshape(ki, 8, BLK)
                values.append(jnp.sum(mine * rrval[:, :, p:p + BLK], axis=0))
            back[:, c * group:(c + 1) * group, :] = jnp.swapaxes(jnp.stack(values), 0, 1)
        start_eight(back_plan)

        for z in range(zblocks):
            p = z * BLK
            index = irow[:, :, :, p:p + BLK].reshape(ki * cells, BLK)
            got = pick(index, index[:, 0:1] // BLK, coarse_two)
            got = got.reshape(ki, cx, cy, BLK) * ival[:, :, :, p:p + BLK]
            field[2, 1:cx + 1, :, p:p + BLK] = (
                field[1, 1:cx + 1, :, p:p + BLK] + jnp.sum(got, axis=0)
            )
        finish_items(first_items)
        finish_eight(slot_plan)
        for t in range(3):
            finish_eight(rim_plan(t))
        wait_eight(back_plan)

        in_place = lanes // 32 == slot_rows % 4

        def spread_some(s, carry):
            p = pl.multiple_of(s * BLK, BLK)
            values = jnp.where(lanes + p < counts[...], turned[s], 0.0)
            high = values.astype(jnp.bfloat16).astype(jnp.float32)
            low = values - high
            turn = ((cell[:, pl.ds(p, BLK)] & (BLK - 1)) // 32 - slot_rows) & 3
            left_side = jnp.concatenate(
                [jnp.where(turn == h, part, 0.0) for part in (high, low) for h in range(4)],
                axis=0,
            ).astype(jnp.bfloat16)
            both = lax.dot_general(
                left_side, hot_spread[s], (((1,), (1,)), ((), ())),
                preferred_element_type=jnp.float32,
            )
            both = both[:32] + both[32:]
            out = jnp.zeros((8, BLK), jnp.float32)
            for h in range(4):
                near = both[8 * h:8 * h + 8]
                near = jnp.where(slot_rows < 4, near[:, :BLK], near[:, BLK:])
                near = jnp.where(in_place, near, 0.0)
                out = out + (pltpu.roll(near, 32 * h, 1) if h else near)
            spread[pl.ds(pl.multiple_of(s * 8, 8), 8)] = out
            return carry

        turned[...] = jnp.swapaxes(returned[...], 0, 1)
        lax.fori_loop(0, slots, spread_some, 0, unroll=32)
        both = jnp.dot(
            choose[...], split_two(spread[...]), preferred_element_type=jnp.float32
        )
        added = both[:, :BLK] + both[:, BLK:]
        for z in range(zblocks):
            p = z * BLK
            field[2, 1:cx + 1, :, p:p + BLK] = (
                field[2, 1:cx + 1, :, p:p + BLK]
                + added[z * cells:(z + 1) * cells].reshape(cx, cy, BLK)
            )
        for i in range(cx):
            put_edges(last_out, 0, i, field[2, i + 1])
        start_items(early_items)
        residual_inside(2)
        for i in range(cx):
            field[3, i + 1] = partial[i]
        smoother_inside(3, 2)
        for i in range(cx):
            put_edges(last_out, 1, i, field[3, i + 1])
            put_edges(last_out, 2, i, partial[i])
        for c in range(4):
            i, j, di, dj = corner_cell(c)
            put_column(tip_out, c, 0, field[2, i + 1][j:j + 1])
            put_column(tip_out, c, zblocks, field[2, i + 1][j + dj:j + dj + 1])
            put_column(tip_out, c, 2 * zblocks, field[2, i + 1 + di][j:j + 1])
            put_column(tip_out, c, 3 * zblocks, field[3, i + 1][j:j + 1])
        start_items(last_items)
        finish_eight(back_plan)
        for t in range(4):
            finish_items(edge_items(t))
            wait_items(edge_items(t))
        wait_items(early_items)
        wait_items(last_items)

        beyond = [layer(last_in, s, 0) for s in range(4)]
        for s in range(4):
            set_ghost(2, s, beyond[s])
        corner_resid = []
        for c in range(4):
            i, j, _, _ = corner_cell(c)
            sx, sy = (0 if i == 0 else 1), (2 if j == 0 else 3)
            value = (
                column(tip_in, c, 3 * zblocks) + beyond[sx][j:j + 1] + beyond[sy][i:i + 1]
            )
            corner_resid.append(jnp.where(exists[CORNERS[c]], value, 0.0))

        for s in range(4):
            low, high = ends[s]
            place = 0 if s % 2 == 0 else cy - 1
            low_side, high_side = (2, 3) if s < 2 else (0, 1)
            change = layer(last_out, s, 0) + at_ends(
                column(tip_in, low, 0), column(tip_in, high, 0)
            )
            beyond_resid = jnp.where(
                side_exists[s], layer(last_in, s, 1) + change, 0.0
            )
            set_ghost(3, s, beyond_resid)
            own_resid = layer(last_out, s, 1) + beyond[s] + at_ends(
                beyond[low_side][place:place + 1], beyond[high_side][place:place + 1]
            )
            wide = (cy, nz)
            before = jnp.where(
                first_row, jnp.broadcast_to(corner_resid[low], wide), pltpu.roll(change, 1, 0)
            )
            after = jnp.where(
                last_row, jnp.broadcast_to(corner_resid[high], wide),
                pltpu.roll(change, cy - 1, 0),
            )
            column_low = zblocks if s >= 2 else 2 * zblocks
            second = at_ends(
                column(ends_in, s, 0) * column(tip_in, low, column_low),
                column(ends_in, s, zblocks) * column(tip_in, high, column_low),
            )
            set_ghost(4, s, (
                layer(last_in, s, 2)
                + edges_in[s, 0] * change
                + edges_in[s, 1] * before
                + edges_in[s, 2] * after
                + layer(first_in, s, 2) * own_resid
                + second
                + edges_in[s, 3] * jnp.where(lane_ids == 0, 0.0, pltpu.roll(change, 1, 1))
                + edges_in[s, 4] * jnp.where(lane_ids == nz - 1, 0.0, pltpu.roll(change, nz - 1, 1))
            ))
        for i in range(cx):
            partial[i] = field[3, i + 1]
        for i in range(cx):
            field[3, i + 1] = residual_row(2, i)
        smoother_inside(3, 2)
        for i in range(cx):
            value = smoother_row(3, i)
            field[4, i + 1] = value
            sol_ref[i] = value
        residual_inside(4)
        for i in range(cx):
            res_ref[i] = residual_row(4, i)

        finish_items(early_items)
        finish_items(last_items)

    f32, i32, bf16 = jnp.float32, jnp.int32, jnp.bfloat16
    vm = pltpu.VMEM
    dma = pltpu.SemaphoreType.DMA
    scratch = [
        vm((ki * 8 * slots, crows), bf16), vm((slots, 256, BLK), bf16), vm((slots, 8, BLK), f32),
        pltpu.SMEM((1, 1, 8), i32), vm((8, BLK), i32),
        vm((5, cx + 2, cy, nz), f32), vm((5, 2, cx, nz), f32),
        vm((cx, cy, nz), f32), vm((cx, cy, nz), f32), vm((6, cx, cy, nz), f32),
        vm((4, 5, 8, nz), f32),
        vm((8, cap), i32), vm((kr, crows, BLK), i32), vm((kr, crows, BLK), f32),
        vm((ka, crows, BLK), i32), vm((crows, BLK), f32), vm((ka, crows, BLK), f32),
        vm((crows, BLK), f32), vm((ka, crows, BLK), f32),
        vm((ki, 8, cap), i32), vm((ki, 8, cap), f32),
        vm((ki, cx, cy, nz), i32), vm((ki, cx, cy, nz), f32),
        vm((cx, cy, nz), f32), vm((fine_rows, 2 * BLK), bf16),
        vm((fine_rows, 8 * slots), bf16),
        vm((8, slots, BLK), f32), vm((8, slots, BLK), f32),
        vm((8, slots, BLK), f32), vm((8, slots, BLK), f32),
        vm((3, crows, BLK), f32), vm((3, 8, rim_rows, BLK), f32),
        vm((8 * slots, BLK), f32), vm((cx, cy, nz), f32),
        vm((4, (3 * 8 + 2) * zblocks, BLK), f32), vm((4, (3 * 8 + 2) * zblocks, BLK), f32),
        vm((4, zblocks, BLK), f32), vm((4, zblocks, BLK), f32),
        vm((4, 3 * 8 * zblocks, BLK), f32), vm((4, 3 * 8 * zblocks, BLK), f32),
        vm((4, 4 * zblocks, BLK), f32), vm((4, 4 * zblocks, BLK), f32),
        vm((4, 5, 8, nz), f32),
        vm((4, 2 * zblocks, BLK), f32), vm((4, 2 * zblocks, BLK), f32),
        dma((27,)), dma((4,)), dma((4,)), dma((4,)), dma((4,)), dma((2, 4)), dma((2, 4)),
        dma((4,)), dma((4,)), dma((4, 4)), dma((4, 4)),
        dma((8,)), dma((8,)), dma((8,)), dma((8,)),
        dma((3, 8)), dma((3, 8)),
    ]
    whole = pl.BlockSpec(memory_space=pltpu.VMEM)
    in_hbm = pl.BlockSpec(memory_space=pltpu.HBM)
    return pl.pallas_call(
        kernel,
        out_shape=(
            jax.ShapeDtypeStruct((cx, cy, nz), f32),
            jax.ShapeDtypeStruct((cx, cy, nz), f32),
        ),
        in_specs=[in_hbm] * 17,
        out_specs=(whole, whole),
        scratch_shapes=scratch,
        compiler_params=pltpu.CompilerParams(
            collective_id=0, has_side_effects=True, vmem_limit_bytes=40 * 1024 * 1024
        ),
        name="vcycle",
    )


def write_out(first, second):
    def kernel(first_ref, second_ref, first_out, second_out, sem):
        copies = [
            pltpu.make_async_copy(first_ref, first_out, sem.at[0]),
            pltpu.make_async_copy(second_ref, second_out, sem.at[1]),
        ]
        for copy in copies:
            copy.start()
        for copy in copies:
            copy.wait()

    return pl.pallas_call(
        kernel,
        out_shape=(
            jax.ShapeDtypeStruct(first.shape, first.dtype),
            jax.ShapeDtypeStruct(second.shape, second.dtype),
        ),
        in_specs=[pl.BlockSpec(memory_space=pltpu.VMEM)] * 2,
        out_specs=(pl.BlockSpec(memory_space=pltpu.HBM),) * 2,
        scratch_shapes=[pltpu.SemaphoreType.DMA((2,))],
        compiler_params=pltpu.CompilerParams(vmem_limit_bytes=4 * 1024 * 1024),
        name="write_out",
    )(first, second)


def body(
    rhs, diag, smoother_center, smoother_faces, send_count, send_cell, restrict_col,
    restrict_vals, coarse_col, coarse_diag, coarse_vals, csmooth_diag, csmooth_vals,
    remote_row, remote_vals, interp_row, interp_vals,
):
    def rows(array):
        return array.reshape(array.shape[0], -1, BLK)

    cap = send_cell.shape[-1]
    ki = remote_row.shape[0]
    def in_hbm(array):
        return pltpu.with_memory_space_constraint(array, pltpu.HBM)

    operands = (
        rhs, diag, smoother_center, smoother_faces,
        send_count,
        send_cell.reshape(8, cap), rows(restrict_col), rows(restrict_vals),
        rows(coarse_col), coarse_diag.reshape(-1, BLK), rows(coarse_vals),
        csmooth_diag.reshape(-1, BLK), rows(csmooth_vals),
        remote_row.reshape(ki, 8, cap), remote_vals.reshape(ki, 8, cap),
        interp_row, interp_vals,
    )
    shapes = {
        "rhs": rhs.shape, "send_cell": (8, cap), "restrict_col": operands[6].shape,
        "coarse_col": operands[8].shape, "interp_row": interp_row.shape,
    }
    sizes = (lax.axis_size("gx"), lax.axis_size("gy"))
    operands = [in_hbm(x) for x in operands]
    return write_out(*make_kernel(sizes, shapes)(*operands))


def solution(mesh):
    fine = P("gx", "gy", None)
    listed = P(None, "gx", "gy", None)
    placed = (
        fine, fine, fine, listed, fine, P("gx", "gy", None, None), listed, listed,
        listed, fine, listed, fine, listed,
        P(None, "gx", "gy", None, None), P(None, "gx", "gy", None, None),
        listed, listed,
    )
    return jax.shard_map(
        body, mesh=mesh, in_specs=placed, out_specs=(fine, fine), check_vma=False
    )
```
